128 devices in a mesh: expert: 32 (over z, y, x_lo), dp: 4 (over x_hi, core).
Axes of the slice: x: 4 (x_hi: 2, x_lo: 2; x = x_hi * 2 + x_lo), y: 4, z: 4, core: 2. Of those that a mesh axis runs over, the one named last changes fastest.
Arguments:
- tokens: bfloat16 [2048, 4096], P(('expert', 'dp')), may hold values from -6 to 6
- expert_ids: int32 [2048, 8], P(('expert', 'dp')), may hold values from 0 to 63, all different within a row; in each aligned block of 16 rows (0 to 15, 16 to 31, ...) at most 4 rows name the same one
- gate_weights: float32 [2048, 8], P(('expert', 'dp')), may hold values from 0.1 to 0.5
- placement: int32 [64], replicated, may hold values from 0 to 63, as said below
- w_gate: bfloat16 [64, 4096, 1536], P('expert', None, 'dp'), may hold values from -0.09375 to 0.09375
- w_up: bfloat16 [64, 4096, 1536], P('expert', None, 'dp'), may hold values from -0.09375 to 0.09375
- w_down: bfloat16 [64, 1536, 4096], P('expert', 'dp'), may hold values from -0.15625 to 0.15625
Outputs:
- mixed: bfloat16 [2048, 4096], P(('expert', 'dp'))
The draws below stay inside these ranges and needn't reach their ends.
Inputs may be any that keep to these rules, and one draw needn't show every extreme that they name: `expert_ids`: each token names 8 different experts; among the 16 tokens of one device no expert is named more than 4 times. `placement`: A permutation of the 64 slots; slot s lies on index s // 2 of the expert axis. The indices of the expert axis are matched in pairs and each pair exchanges one expert; every other expert e sits in slot e.
All inputs are finite; a program needn't handle non-finite values.
Results may differ from the reference program's by a relative error of at most 0.014.
Values may be sent and summed in bfloat16 or wider, within the bound.
No kernel may reach another device: no remote copies, remote signals or barrier semaphores. Data moves between devices by JAX's collectives and lax.ppermute only.
A program may use at most 128 MiB of HBM per device.

```python
import math
import jax
import jax.numpy as jnp
import numpy as np
from jax import lax

D = 4096
FF = 1536
TOP = 8
EXP_DEV = 2
TOK_DEV = 16
EXPERTS = 64
CAP = 4
TOKENS = 2048
N_DP = 4


def draw_placement(key, part):
    key = jax.random.fold_in(key, 11)
    key_order, key_first, key_second = jax.random.split(key, 3)
    devices = EXPERTS // EXP_DEV
    order = jax.random.permutation(key_order, devices).astype(jnp.int32)
    first = order[0::2]
    second = order[1::2]
    local_first = jax.random.randint(key_first, (devices // 2,), 0, EXP_DEV).astype(jnp.int32)
    local_second = jax.random.randint(key_second, (devices // 2,), 0, EXP_DEV).astype(jnp.int32)
    expert_first = first * EXP_DEV + local_first
    expert_second = second * EXP_DEV + local_second
    base = jnp.arange(EXPERTS, dtype=jnp.int32)
    return base.at[expert_first].set(expert_second).at[expert_second].set(expert_first)


def block_levels(own_key, shape, cuts, smallest, top_value):
    factor_of, own = 1.0, jax.random.fold_in(own_key, 6)
    for position, blocks in cuts:
        heights = jnp.exp(jax.random.uniform(jax.random.fold_in(own, position), (blocks,), jnp.float32, smallest / len(cuts), top_value / len(cuts)))
        factor_of = factor_of * jnp.repeat(heights, shape[position] // blocks).reshape([-1 if axis == position else 1 for axis in range(len(shape))])
    return factor_of


def shared_out(rng, own, number, rows, number_of, top, limit, lean):
    sequence = jax.random.permutation(rng, number_of)
    heavy_load, usual = portions_of(number_of, rows * top, limit, lean, True), portions_of(number_of, rows * top, limit, lean, False)
    places = jnp.arange(number_of)

    def named(lengths, turn):
        used = int((lengths > 0).sum())
        fixed = max(1, used // 4)
        shifted = fixed + (places - fixed + turn * (used - fixed)) % max(1, number_of - fixed)
        return jnp.zeros((number_of,), jnp.int32).at[sequence[jnp.where(places < fixed, places, shifted)]].set(jnp.asarray(lengths, jnp.int32))

    lengths = jnp.where(number % 4 == 0, named(heavy_load, number // 4), named(usual, number - number // 4 - 1))
    mixed = jax.random.permutation(jax.random.fold_in(own, 3), number_of)
    source_of, taker = mixed[0:number_of // 2 * 2:2], mixed[1:number_of // 2 * 2:2]
    slack = jnp.minimum(lengths[source_of] - 1, limit - lengths[taker]) // 2
    slack = jnp.where((source_of == sequence[0]) | (taker == sequence[0]) | (lengths[taker] == 0), 0, jnp.maximum(slack, 0))
    shifted = jax.random.randint(jax.random.fold_in(own, 4), (number_of // 2,), 0, 1 << 20) % (slack + 1)
    lengths = lengths.at[source_of].add(-shifted).at[taker].add(shifted)
    items = jnp.searchsorted(jnp.cumsum(lengths), jnp.arange(rows * top), side="right").astype(jnp.int32)
    grid = items.reshape(top, rows).T
    grid = grid[jax.random.permutation(jax.random.fold_in(own, 1), rows)]
    turn = jax.random.randint(jax.random.fold_in(own, 2), (rows, 1), 0, top)
    return jnp.take_along_axis(grid, (jnp.arange(top)[None, :] + turn) % top, axis=1)


def portions_of(amount, total, limit, slope, full):
    loads = [(1 << 20) // math.isqrt(standing ** slope) + 1 for standing in range(1, amount + 1)]
    largest = limit if full else min(limit, max(-(-total // amount), total * loads[0] // sum(loads)))
    least = 1 if total - largest >= amount - 1 else 0
    holding, surplus = [largest] + [least] * (amount - 1), total - largest - least * (amount - 1)
    while surplus > 0:
        free = [i for i in range(1, amount) if holding[i] < largest] or [i for i in range(1, amount) if holding[i] < limit]
        mass, remaining = sum([loads[i] for i in free]), surplus
        for i in free:
            more = min(limit - holding[i], max(1, remaining * loads[i] // mass), surplus)
            holding[i] = holding[i] + more
            surplus = surplus - more
    return np.array(holding)


def centred(stream_key, extent, scale, reach, cuts=(), kind=jnp.bfloat16):
    drawn = scale * jax.random.normal(stream_key, extent, jnp.float32)
    if cuts:
        drawn = drawn * block_levels(stream_key, extent, cuts, -0.22, 0.18)
    return jnp.clip(drawn, -reach, reach).astype(kind)


def setup_inputs(seed: int = 0) -> dict:
    splits = jax.random.split(jax.random.key(seed), 8)
    tokens = centred(splits[0], (TOKENS, D), 1.0, 6.0, ((0, 128),))
    expert_ids_keys = jax.random.split(jax.random.fold_in(splits[1], 1), TOKENS // TOK_DEV)
    expert_ids_turns = jax.random.permutation(jax.random.fold_in(splits[1], 3), TOKENS // TOK_DEV)
    expert_ids = jax.vmap(lambda own, number: shared_out(jax.random.fold_in(splits[1], 2), own, number, TOK_DEV, EXPERTS, TOP, CAP, 2))(expert_ids_keys, expert_ids_turns).reshape((TOKENS, TOP))
    gate_weights = jnp.clip(0.1 + 0.4 * jax.random.uniform(splits[2], (TOKENS, TOP), jnp.float32) ** block_levels(splits[2], (TOKENS, TOP), ((0, 128),), -0.2, 0.2), 0.1, 0.5)
    placement = draw_placement(jax.random.fold_in(splits[7], 71), 0)
    w_gate = centred(splits[4], (EXPERTS, D, FF), D ** -0.5, 0.09375, ((0, 32), (2, 4)))
    w_up = centred(splits[5], (EXPERTS, D, FF), D ** -0.5, 0.09375, ((0, 32), (2, 4)))
    w_down = centred(splits[6], (EXPERTS, FF, D), FF ** -0.5, 0.15625, ((0, 32), (1, 4)))
    return {"tokens": tokens, "expert_ids": expert_ids, "gate_weights": gate_weights, "placement": placement, "w_gate": w_gate, "w_up": w_up, "w_down": w_down}


def reference(tokens, expert_ids, gate_weights, placement, w_gate, w_up, w_down):
    slot_of = placement[expert_ids.reshape(-1)]
    order = jnp.argsort(slot_of, stable=True).astype(jnp.int32)
    counts = jnp.sum((slot_of[:, None] == jnp.arange(EXPERTS, dtype=jnp.int32)[None, :]).astype(jnp.int32), axis=0)
    starts = (jnp.cumsum(counts) - counts).astype(jnp.int32)
    longest = (TOKENS // TOK_DEV) * CAP
    padded = jnp.concatenate([order, jnp.zeros((longest,), jnp.int32)])
    flat_gates = gate_weights.reshape(-1)

    def visit(total, slot):
        picked = lax.dynamic_slice_in_dim(padded, starts[slot], longest)
        valid = jnp.arange(longest, dtype=jnp.int32) < counts[slot]
        row_tok = picked // TOP
        weight = jnp.where(valid, flat_gates[picked], jnp.zeros_like(flat_gates[picked]))
        rows_in = tokens[row_tok]
        gate = jnp.dot(rows_in, w_gate[slot], preferred_element_type=jnp.float32)
        up = jnp.dot(rows_in, w_up[slot], preferred_element_type=jnp.float32)
        hidden = (jax.nn.silu(gate) * up).astype(jnp.bfloat16)
        quarters = hidden.reshape(longest, N_DP, FF // N_DP).astype(jnp.float32)
        down = w_down[slot].reshape(N_DP, FF // N_DP, D).astype(jnp.float32)
        parts = jnp.einsum("rqf,qfd->qrd", quarters, down)
        rounded = lax.optimization_barrier(parts.astype(jnp.bfloat16)).astype(jnp.float32)
        expert_out = jnp.sum(rounded, axis=0).astype(jnp.bfloat16)
        total = total.at[row_tok].add(weight[:, None] * expert_out.astype(jnp.float32))
        return total, None

    total, unused = lax.scan(visit, jnp.zeros((TOKENS, D), jnp.float32), jnp.arange(EXPERTS, dtype=jnp.int32))
    return total.astype(jnp.bfloat16)
```

```python
import jax
import jax.numpy as jnp
from jax import lax
from jax.sharding import PartitionSpec as P

AXES = ("expert", "dp")
SIDE = 4
META = 128
FIRST, SECOND = (1, 3), (3, 1)


def partners(axis, masks):
    pairs = []
    for z in range(SIDE):
        for y in range(SIDE):
            for x in range(SIDE):
                for core in range(2):
                    other, to_core = [z, y, x], core
                    if axis == "core":
                        to_core = 1 - core
                    else:
                        other["zyx".index(axis)] ^= masks[core]
                    pairs.append((place(z, y, x, core), place(*other, to_core)))
    return pairs


def place(z, y, x, core):
    return ((z * SIDE + y) * 2 + x % 2) * 4 + (x // 2) * 2 + core


def swap(value, axis, masks=None):
    return lax.ppermute(value, AXES, partners(axis, masks))


def gather_line(value, axis):
    pair = jnp.stack([value, swap(value, axis, FIRST)])
    return jnp.concatenate([pair, swap(pair, axis, SECOND)])


def sum_line(value, axis):
    here = value[:2] + swap(value[2:].astype(jnp.bfloat16), axis, SECOND).astype(jnp.float32)
    return here[0] + swap(here[1].astype(jnp.bfloat16), axis, FIRST).astype(jnp.float32)


def chooser(rows, slots, half, tok_count, cap):
    count = rows.shape[0]
    named_slots = rows[:, half : half + 8].astype(jnp.float32).astype(jnp.int32)
    named = jnp.any(named_slots[None] == slots[:, None, None], axis=2)
    grouped = named.reshape(slots.shape[0], -1, tok_count)
    earlier = jnp.arange(tok_count)[:, None] > jnp.arange(tok_count)[None, :]
    rank = jnp.sum((grouped[:, :, None, :] & earlier[None, None]).astype(jnp.int32), axis=3)
    rank = jnp.where(grouped, rank, -1).reshape(slots.shape[0], count)
    lines = (count // tok_count) * cap
    line = jnp.arange(lines, dtype=jnp.int32)
    block = jnp.arange(count, dtype=jnp.int32) // tok_count
    hit = (rank[:, None, :] == (line % cap)[None, :, None]) & (block[None, :] == (line // cap)[:, None])[None]
    return hit.reshape(slots.shape[0] * lines, count).astype(jnp.bfloat16)


def shards(tokens, expert_ids, gate_weights, placement, w_gate, w_up, w_down):
    tok_count, width = tokens.shape
    top_count = expert_ids.shape[1]
    per_device = w_gate.shape[0]
    half = width // 2
    cap = 4
    core = lax.axis_index("dp") % 2
    own_slot = lax.axis_index("expert") * per_device
    mask_1 = jnp.where(core == 0, FIRST[0], FIRST[1])
    mask_2 = jnp.where(core == 0, SECOND[0], SECOND[1])

    slot_range = jnp.arange(placement.shape[0], dtype=jnp.int32)
    slot_of = jnp.sum((expert_ids[:, :, None] == slot_range) * placement, axis=2)
    high = lax.reduce_precision(gate_weights, 8, 7)
    middle = lax.reduce_precision(gate_weights - high, 8, 7)
    low = gate_weights - high - middle
    meta = jnp.concatenate([slot_of.astype(jnp.float32), high, middle, low], axis=1)
    meta = jnp.pad(meta, ((0, 0), (0, META - 4 * top_count))).astype(jnp.bfloat16)
    extended = jnp.concatenate([tokens[:, :half], meta, tokens[:, half:]], axis=1)

    near = gather_line(extended, "z").reshape(SIDE * tok_count, width + META)
    plane_a = gather_line(near[:, : half + META], "y").reshape(-1, half + META)
    plane_b = gather_line(
        jnp.concatenate([near[:, half + META :], near[:, half : half + META]], axis=1), "x"
    ).reshape(-1, half + META)

    local = jnp.arange(per_device, dtype=jnp.int32)
    arrived, choosers = [], []
    for plane, axis, bit in ((plane_a, "x", 2), (plane_b, "y", 4)):
        masks = jnp.stack([mask_1, jnp.int32(2), mask_2, jnp.int32(0)])
        moved = (masks & 1) * 2 if axis == "x" else masks * 4
        slots = ((own_slot ^ moved)[:, None] + local[None, :]).reshape(-1)
        choose = chooser(plane, slots, half, tok_count, cap)
        packed = jnp.dot(choose, plane, preferred_element_type=jnp.bfloat16)
        quarter = packed.shape[0] // 4
        got_1 = swap(packed[: 2 * quarter], axis, FIRST)
        send_2 = jnp.concatenate([packed[2 * quarter : 3 * quarter], got_1[quarter:]])
        got_2 = swap(send_2, axis, SECOND)
        mine = jnp.concatenate([packed[3 * quarter :], got_1[:quarter], got_2])
        arrived.append(mine.reshape(SIDE, per_device, SIDE, -1, half + META))
        choosers.append(choose)
    own_a = arrived[0].transpose(1, 0, 2, 3, 4)
    own_b = arrived[1].transpose(1, 2, 0, 3, 4)
    granule = own_a.shape[3]
    own_a = own_a.reshape(per_device, -1, half + META)
    own_b = own_b.reshape(per_device, -1, half + META)[:, :, :half]
    sets = ((own_a, own_b), (swap(own_a, "core"), swap(own_b, "core")))

    scaled = []
    for rows_a, rows_b in sets:
        info = rows_a[:, :, half:].astype(jnp.float32)
        named = info[:, :, :top_count].astype(jnp.int32) == (own_slot + local)[:, None, None]
        parts = [info[:, :, k * top_count : (k + 1) * top_count] for k in (1, 2, 3)]
        weight = jnp.sum(jnp.where(named, parts[0] + parts[1] + parts[2], 0.0), axis=2)

        def project(w):
            return jnp.einsum(
                "ltd,ldf->ltf", rows_a[:, :, :half], w[:, :half], preferred_element_type=jnp.float32
            ) + jnp.einsum("ltd,ldf->ltf", rows_b, w[:, half:], preferred_element_type=jnp.float32)

        hidden = (jax.nn.silu(project(w_gate)) * project(w_up)).astype(jnp.bfloat16)
        scaled.append((hidden, weight[:, :, None]))

    def down(which, columns):
        hidden, weight = scaled[which]
        return weight * jnp.einsum(
            "ltf,lfd->ltd", hidden, w_down[:, :, columns], preferred_element_type=jnp.float32
        )

    sums = []
    for index, axis, line, columns in ((0, "x", "y", slice(0, half)), (1, "y", "x", slice(half, None))):
        other = swap(down(1, columns).astype(jnp.bfloat16), "core")
        both = (down(0, columns) + other.astype(jnp.float32)).astype(jnp.bfloat16)
        both = both.reshape(per_device, SIDE, SIDE, granule, half)
        both = both.transpose((1, 0, 2, 3, 4) if axis == "x" else (2, 0, 1, 3, 4))
        both = both.reshape(SIDE, -1, half)
        quarter = both.shape[1]
        back_2 = swap(both[2:].reshape(-1, half), axis, SECOND)
        back_1 = swap(jnp.concatenate([both[1], back_2[quarter:]]), axis, FIRST)
        values = jnp.concatenate([back_1, back_2[:quarter], both[0]])
        dense = lax.dot_general(
            choosers[index], values, (((0,), (0,)), ((), ())), preferred_element_type=jnp.float32
        )
        sums.append(sum_line(dense.reshape(SIDE, -1, half), line))
    total = jnp.concatenate(sums, axis=1).reshape(SIDE, tok_count, width)
    return sum_line(total, "z").astype(jnp.bfloat16)


def solution(mesh):
    in_specs = (
        P(AXES, None),
        P(AXES, None),
        P(AXES, None),
        P(),
        P("expert", None, "dp"),
        P("expert", None, "dp"),
        P("expert", "dp", None),
    )
    return jax.shard_map(shards, mesh=mesh, in_specs=in_specs, out_specs=P(AXES, None), check_vma=False)
```

```python
import functools

import jax
import jax.numpy as jnp
from jax import lax
from jax.experimental import pallas as pl
from jax.experimental.pallas import tpu as pltpu
from jax.sharding import PartitionSpec as P

AXES = ("expert", "dp")
SIDE = 4
META = 128
CAP = 4
PARTS = 2


def place(z, y, x, core):
    return ((z * SIDE + y) * 2 + x % 2) * 4 + (x // 2) * 2 + core


def partners(axes, mask):
    pairs = []
    for z in range(SIDE):
        for y in range(SIDE):
            for x in range(SIDE):
                for core in range(2):
                    other = [z, y, x]
                    other["zyx".index(axes[core])] ^= mask
                    pairs.append((place(z, y, x, core), place(*other, core)))
    return pairs


def exchange(value, axes):
    return [value[0]] + [lax.ppermute(value[j], AXES, partners(axes, j)) for j in (1, 2, 3)]


def gather_line(value, axes):
    return jnp.stack(exchange([value] * SIDE, axes))


def sum_line(value, axes):
    sent = value.astype(jnp.bfloat16)
    pieces = exchange([value[0], sent[1], sent[2], sent[3]], axes)
    return (pieces[0] + pieces[1].astype(jnp.float32)) + (pieces[2].astype(jnp.float32) + pieces[3].astype(jnp.float32))


def sibling(value):
    pairs = [(i, i ^ 1) for i in range(SIDE**3 * 2)]
    return lax.ppermute(value, AXES, pairs)


def pack_kernel(wanted_ref, *refs, top, tok_count, step):
    planes, outs, choice_ref = refs[:SIDE], refs[SIDE:-1], refs[-1]
    wanted = wanted_ref[...]
    tokens, lines = planes[0].shape[0], wanted.shape[1]
    blocks = tokens // tok_count
    token_block = lax.broadcasted_iota(jnp.int32, (tokens, lines), 0) // tok_count
    line_block = lax.broadcasted_iota(jnp.int32, (tokens, lines), 1) // CAP % blocks
    inside = token_block == line_block
    share = lines // SIDE
    for p in range(SIDE):
        codes = planes[p][:, PARTS * step :].astype(jnp.float32)
        found = codes[:, :1] == wanted
        for k in range(1, top):
            found = found | (codes[:, k : k + 1] == wanted)
        choice = jnp.where(found & inside, 1.0, 0.0)
        choice_ref[p] = choice.astype(jnp.bfloat16)
        take = choice.T.astype(jnp.bfloat16)
        for part in range(PARTS):
            end = (part + 1) * step if part < PARTS - 1 else planes[p].shape[1]
            rows = jnp.dot(take, planes[p][:, part * step : end], preferred_element_type=jnp.float32)
            rows = rows.astype(jnp.bfloat16)
            for j in range(SIDE):
                out = outs[part * SIDE + j]
                out[p] = rows[j * share : (j + 1) * share].reshape(out.shape[1:])


def gate_kernel(base_ref, *refs, sources, step, has_total, weigh, finish):
    refs = list(refs)
    slot_ref = refs.pop(0) if weigh else None
    pieces = [[refs.pop(0) for _ in range(SIDE)] for _ in sources]
    weights = [(refs.pop(0), refs.pop(0)) for _ in sources]
    total_in = refs.pop(0) if has_total else None
    total_ref = refs.pop(0)
    weight_ref = refs.pop(0) if weigh else None
    [rows_ref] = refs
    granule, columns = pieces[0][0].shape[2], weights[0][0].shape[2]
    gate = up = None
    for source, held, (gate_w, up_w) in zip(sources, pieces, weights):
        for last in range(SIDE):
            for plane in range(SIDE):
                piece = held[last][plane, 0] if source == "own" else held[plane][last, 0]
                line = (last * SIDE + plane) * granule
                rows_ref[line : line + granule] = piece[:, :step]
                if weigh:
                    info = piece[:, step:].astype(jnp.float32)
                    code = CAP * (slot_ref[0] + pl.program_id(0)).astype(jnp.float32)
                    named = (info >= code) & (info < code + CAP) & (lax.broadcasted_iota(jnp.int32, info.shape, 1) < META // 2)
                    value = pltpu.roll(info, META // 2, 1)
                    weight_ref[0, line : line + granule] = jnp.sum(jnp.where(named, value, 0.0), axis=1, keepdims=True)
        rows = rows_ref[...]
        one = jnp.dot(rows, gate_w[0], preferred_element_type=jnp.float32)
        two = jnp.dot(rows, up_w[0], preferred_element_type=jnp.float32)
        gate, up = (one, two) if gate is None else (gate + one, up + two)
    if has_total:
        gate, up = gate + total_in[0, :, :columns], up + total_in[0, :, columns:]
    if finish:
        total_ref[0] = (jax.nn.silu(gate) * up).astype(jnp.bfloat16)
    else:
        total_ref[0, :, :columns] = gate
        total_ref[0, :, columns:] = up


def down_kernel(base_ref, hidden_ref, weight_ref, w_ref, *refs, turned):
    outs, added = refs[-SIDE:], refs[:-SIDE]
    granule = outs[0].shape[2]
    value = weight_ref[0] * jnp.dot(hidden_ref[0], w_ref[0], preferred_element_type=jnp.float32)
    for last in range(SIDE):
        for plane in range(SIDE):
            line = (last * SIDE + plane) * granule
            rows = value[line : line + granule]
            if turned:
                outs[plane][last, 0] = rows.astype(jnp.bfloat16)
            else:
                outs[last][plane, 0] = (rows + added[last][plane, 0].astype(jnp.float32)).astype(jnp.bfloat16)


def unpack_kernel(choice_ref, *refs):
    pieces, outs = refs[:SIDE], refs[SIDE:]
    for p in range(SIDE):
        values = jnp.concatenate([piece[p].reshape(-1, piece.shape[3]) for piece in pieces])
        dense = jnp.dot(choice_ref[p], values, preferred_element_type=jnp.float32)
        outs[p][...] = dense.astype(outs[p].dtype)


def whole(count):
    return [pl.BlockSpec(memory_space=pltpu.VMEM)] * count


def params():
    return pltpu.CompilerParams(vmem_limit_bytes=48 * 2**20)


def cost(flops, read):
    return pl.CostEstimate(flops=int(flops), bytes_accessed=int(read), transcendentals=0)


def shards(tokens, expert_ids, gate_weights, placement, w_gate, w_up, w_down):
    tok_count, width = tokens.shape
    top = expert_ids.shape[1]
    per_device = w_gate.shape[0]
    half = width // 2
    core = lax.axis_index("dp") % 2
    first_core = core == 0
    own_slot = lax.axis_index("expert") * per_device
    local = jnp.arange(per_device, dtype=jnp.int32)

    slot_range = jnp.arange(placement.shape[0], dtype=jnp.int32)
    slot_of = jnp.sum((expert_ids[:, :, None] == slot_range) * placement, axis=2)
    same = jnp.any(slot_of[:, :, None, None] == slot_of[None, None], axis=3)
    earlier = jnp.arange(tok_count)[:, None] > jnp.arange(tok_count)[None, :]
    rank = jnp.sum((same & earlier[:, None, :]).astype(jnp.int32), axis=2)
    code = (slot_of * CAP + rank).astype(jnp.float32)
    high = lax.reduce_precision(gate_weights, 8, 7)
    middle = lax.reduce_precision(gate_weights - high, 8, 7)
    low = gate_weights - high - middle
    gap = jnp.full((tok_count, META // 2 - 3 * top), -1.0)
    meta = jnp.concatenate([code, code, code, gap, high, middle, low, gap], axis=1).astype(jnp.bfloat16)
    left, right = tokens[:, :half], tokens[:, half:]
    kept = jnp.concatenate([jnp.where(first_core, left, right), meta], axis=1)
    got = sibling(jnp.concatenate([jnp.where(first_core, right, left), meta], axis=1))
    both = jnp.concatenate([jnp.where(first_core, kept, got), jnp.where(first_core, got, kept)])

    near = gather_line(both, "zz").reshape(-1, META + half)
    planes = exchange([near] * SIDE, "yx")

    step = half // PARTS
    lines = near.shape[0] // tok_count * CAP * per_device * SIDE
    masks = jnp.arange(SIDE, dtype=jnp.int32)
    moved = jnp.where(first_core, (masks & 1) * 2, masks * 4)
    slots = ((own_slot ^ moved)[:, None] + local[None, :]).reshape(-1)
    wanted = slots[:, None, None] * CAP + jnp.zeros((1, near.shape[0] // tok_count, 1), jnp.int32) + jnp.arange(CAP, dtype=jnp.int32)
    wanted = wanted.astype(jnp.float32).reshape(1, lines)
    granule = near.shape[0] // tok_count * CAP
    rows_of = lambda columns: jax.ShapeDtypeStruct((SIDE, per_device, granule, columns), jnp.bfloat16)
    widths = [step] * (PARTS - 1) + [step + META]
    *packed, choice = pl.pallas_call(
        functools.partial(pack_kernel, top=top, tok_count=tok_count, step=step),
        out_shape=[rows_of(w) for w in widths for _ in range(SIDE)]
        + [jax.ShapeDtypeStruct((SIDE, near.shape[0], lines), jnp.bfloat16)],
        in_specs=whole(1 + SIDE),
        out_specs=whole(PARTS * SIDE + 1),
        compiler_params=params(),
    )(wanted, *planes)

    base = jnp.stack([core * PARTS, (1 - core) * PARTS]).astype(jnp.int32)
    rows_count, hidden_count = SIDE * SIDE * granule, w_gate.shape[2]

    def piece_spec(columns):
        return pl.BlockSpec((SIDE, 1, granule, columns), lambda slot, *_: (0, slot, 0, 0))

    def slot_spec(columns):
        return pl.BlockSpec((1, rows_count, columns), lambda slot, *_: (slot, 0, 0))

    def project(sources, part, total, weigh, finish):
        names = tuple(sources)
        in_specs = [piece_spec(widths[part])] * (SIDE * len(names))
        operands = [p for name in names for p in sources[name]]
        for name in names:
            which = 0 if name == "own" else 1
            spec = pl.BlockSpec((1, step, hidden_count), lambda slot, base, *_, which=which: (slot, base[which] + part, 0))
            in_specs += [spec, spec]
            operands += [w_gate, w_up]
        if total is not None:
            in_specs.append(slot_spec(2 * hidden_count))
            operands.append(total)
        if finish:
            out_shape = [jax.ShapeDtypeStruct((per_device, rows_count, hidden_count), jnp.bfloat16)]
            out_specs = [slot_spec(hidden_count)]
        else:
            out_shape = [jax.ShapeDtypeStruct((per_device, rows_count, 2 * hidden_count), jnp.float32)]
            out_specs = [slot_spec(2 * hidden_count)]
        if weigh:
            out_shape.append(jax.ShapeDtypeStruct((per_device, rows_count, 1), jnp.float32))
            out_specs.append(slot_spec(1))
        scalars = [base] + ([own_slot.reshape(1)] if weigh else [])
        return pl.pallas_call(
            functools.partial(gate_kernel, sources=names, step=step, has_total=total is not None, weigh=weigh, finish=finish),
            grid_spec=pltpu.PrefetchScalarGridSpec(
                num_scalar_prefetch=len(scalars),
                grid=(per_device,),
                in_specs=in_specs,
                out_specs=out_specs,
                scratch_shapes=[pltpu.VMEM((rows_count, step), jnp.bfloat16)],
            ),
            out_shape=out_shape,
            compiler_params=params(),
            cost_estimate=cost(len(names) * 4 * per_device * rows_count * step * hidden_count, 8e6),
        )(*scalars, *operands)

    arrived = []
    for part in range(PARTS):
        own = exchange(packed[part * SIDE : (part + 1) * SIDE], "xy")
        arrived.append((own, [sibling(piece) for piece in own]))
    [total] = project({"own": arrived[0][0], "sibling": arrived[0][1]}, 0, None, False, False)
    total, weight = project({"own": arrived[1][0]}, 1, total, True, False)
    [hidden] = project({"sibling": arrived[1][1]}, 1, total, False, True)

    def down(part, turned, added):
        spec = piece_spec(step)
        which = 1 if turned else 0
        return pl.pallas_call(
            functools.partial(down_kernel, turned=turned),
            grid_spec=pltpu.PrefetchScalarGridSpec(
                num_scalar_prefetch=1,
                grid=(per_device,),
                in_specs=[
                    slot_spec(hidden_count),
                    slot_spec(1),
                    pl.BlockSpec((1, hidden_count, step), lambda slot, base: (slot, 0, base[which] + part)),
                ]
                + [spec] * len(added),
                out_specs=[spec] * SIDE,
            ),
            out_shape=[rows_of(step)] * SIDE,
            compiler_params=params(),
            cost_estimate=cost(2 * per_device * rows_count * step * hidden_count, 5e6),
        )(base, hidden, weight, w_down, *added)

    sums = []
    for part in range(PARTS):
        added = [sibling(piece) for piece in down(part, True, [])]
        values = exchange(down(part, False, added), "xy")
        kinds = [jnp.float32] + [jnp.bfloat16] * (SIDE - 1)
        dense = pl.pallas_call(
            unpack_kernel,
            out_shape=[jax.ShapeDtypeStruct((near.shape[0], step), kind) for kind in kinds],
            in_specs=whole(1 + SIDE),
            out_specs=whole(SIDE),
            compiler_params=params(),
        )(choice, *values)
        sums.append(sum(piece.astype(jnp.float32) for piece in exchange(dense, "yx")))
    total = jnp.concatenate(sums, axis=1).reshape(SIDE, -1, half)
    total = sum_line(total, "zz").astype(jnp.bfloat16).reshape(2, tok_count, half)
    kept = jnp.where(first_core, total[0], total[1])
    got = sibling(jnp.where(first_core, total[1], total[0]))
    return jnp.concatenate([jnp.where(first_core, kept, got), jnp.where(first_core, got, kept)], axis=1)


def solution(mesh):
    in_specs = (
        P(AXES, None),
        P(AXES, None),
        P(AXES, None),
        P(),
        P("expert", None, "dp"),
        P("expert", None, "dp"),
        P("expert", "dp", None),
    )
    return jax.shard_map(shards, mesh=mesh, in_specs=in_specs, out_specs=P(AXES, None), check_vma=False)
```

```python
import functools

import jax
import jax.numpy as jnp
from jax import lax
from jax.experimental import pallas as pl
from jax.experimental.pallas import tpu as pltpu
from jax.sharding import PartitionSpec as P

AXES = ("expert", "dp")
SIDE = 4
META = 128
CAP = 4
PARTS = 1
BACK = 2


def place(z, y, x, core):
    return ((z * SIDE + y) * 2 + x % 2) * 4 + (x // 2) * 2 + core


def partners(axes, masks):
    masks = (masks, masks) if isinstance(masks, int) else masks
    pairs = []
    for z in range(SIDE):
        for y in range(SIDE):
            for x in range(SIDE):
                for core in range(2):
                    other = [z, y, x]
                    other["zyx".index(axes[core])] ^= masks[core]
                    pairs.append((place(z, y, x, core), place(*other, core)))
    return pairs


def exchange(value, axes):
    over = lax.ppermute(value[2], AXES, partners(axes, 2))
    one, three = (lax.ppermute(value[j], AXES, partners(axes, j)) for j in (1, 3))
    return [value[0], one, over, three]


def exchange_z(value, first_core):
    over = lax.ppermute(value[2], AXES, partners("zz", 2))
    near = lax.ppermute(jnp.where(first_core, value[1], value[3]), AXES, partners("zz", (1, 3)))
    far = lax.ppermute(jnp.where(first_core, value[3], value[1]), AXES, partners("zz", (3, 1)))
    return [value[0], jnp.where(first_core, near, far), over, jnp.where(first_core, far, near)]


def sibling(value):
    pairs = [(i, i ^ 1) for i in range(SIDE**3 * 2)]
    return lax.ppermute(value, AXES, pairs)


def prepare_kernel(core_ref, tokens_ref, ids_ref, weights_ref, placement_ref, kept_ref, sent_ref):
    top, count = ids_ref.shape
    width = tokens_ref.shape[1]
    half, step = width // 2, width // 2 // PARTS
    slot_count = placement_ref.shape[1]
    lanes = lax.broadcasted_iota(jnp.int32, (count, slot_count), 1)
    placement = placement_ref[...].astype(jnp.float32)
    line = lax.broadcasted_iota(jnp.int32, (count, count), 0)
    column = lax.broadcasted_iota(jnp.int32, (count, count), 1)
    diagonal = line == column
    slots = []
    named = jnp.zeros((count, slot_count), jnp.float32)
    for k in range(top):
        ids = jnp.sum(jnp.where(diagonal, ids_ref[k : k + 1], 0), axis=1, keepdims=True)
        slot = jnp.sum(jnp.where(ids == lanes, placement, 0.0), axis=1, keepdims=True)
        slots.append(slot)
        named = jnp.where(lanes.astype(jnp.float32) == slot, 1.0, named)
    before = jnp.where(line > column, 1.0, 0.0)
    ranks = jnp.dot(before.astype(jnp.bfloat16), named.astype(jnp.bfloat16), preferred_element_type=jnp.float32)
    lane = lax.broadcasted_iota(jnp.int32, (count, META), 1)
    meta = jnp.full((count, META), -1.0, jnp.float32)
    for k in range(top):
        rank = jnp.sum(jnp.where(lanes.astype(jnp.float32) == slots[k], ranks, 0.0), axis=1, keepdims=True)
        weight = jnp.sum(jnp.where(diagonal, weights_ref[k : k + 1], 0.0), axis=1, keepdims=True)
        high = weight.astype(jnp.bfloat16).astype(jnp.float32)
        middle = (weight - high).astype(jnp.bfloat16).astype(jnp.float32)
        for turn, term in enumerate((high, middle, weight - high - middle)):
            at = turn * top + k
            meta = jnp.where(lane == at, slots[k] * CAP + rank, meta)
            meta = jnp.where(lane == META // 2 + at, term, meta)
    meta = meta.astype(jnp.bfloat16)
    for ref, own in ((kept_ref, True), (sent_ref, False)):
        begin = core_ref[0] * half if own else half - core_ref[0] * half
        begin = pl.multiple_of(begin, 128)
        ref[:, :step] = tokens_ref[:, pl.ds(begin, step)]
        ref[:, step : step + META] = meta
        if step < half:
            ref[:, step + META :] = tokens_ref[:, pl.ds(pl.multiple_of(begin + step, 128), half - step)]


def fetch_kernel(gate_ref, up_ref, both_ref, sems):
    columns = gate_ref.shape[2]
    copies = [
        pltpu.make_async_copy(ref, both_ref.at[:, :, pl.ds(i * columns, columns)], sems.at[i])
        for i, ref in enumerate((gate_ref, up_ref))
    ]
    for copy in copies:
        copy.start()
    for copy in copies:
        copy.wait()


def pack_kernel(*refs, top, tok_count, step, first):
    wanted_ref, planes, outs = refs[0], refs[1 : 1 + SIDE], refs[1 + SIDE : 1 + 2 * SIDE]
    if first:
        choice_ref = refs[-1]
        wanted = wanted_ref[...]
        tokens, lines = planes[0].shape[0], wanted.shape[1]
        blocks = tokens // tok_count
        token_block = lax.broadcasted_iota(jnp.int32, (tokens, lines), 0) // tok_count
        line_block = lax.broadcasted_iota(jnp.int32, (tokens, lines), 1) // CAP % blocks
        inside = token_block == line_block
    for p in range(SIDE):
        if first:
            codes = planes[p][:, step : step + META].astype(jnp.float32)
            found = codes[:, :1] == wanted
            for k in range(1, top):
                found = found | (codes[:, k : k + 1] == wanted)
            choice = jnp.where(found & inside, 1.0, 0.0)
            choice_ref[p] = choice.astype(jnp.bfloat16)
        else:
            choice = wanted_ref[p].astype(jnp.float32)
        take = choice.T.astype(jnp.bfloat16)
        rows = jnp.dot(take, planes[p][...], preferred_element_type=jnp.float32).astype(jnp.bfloat16)
        share = rows.shape[0] // SIDE
        for j in range(SIDE):
            outs[j][p] = rows[j * share : (j + 1) * share].reshape(outs[j].shape[1:])


def gate_kernel(base_ref, *refs, source, part, weigh, has_total, finish):
    refs = list(refs)
    pieces = [refs.pop(0) for _ in range(SIDE)]
    w_ref = refs.pop(0)
    total_in = refs.pop(0) if has_total else None
    total_ref = refs.pop(0)
    weight_ref = refs.pop(0) if weigh else None
    [rows_ref] = refs
    granule, columns = pieces[0].shape[2], w_ref.shape[2] // 2
    step = rows_ref.shape[1]
    which = 0 if source == "own" else 1
    begin = pl.multiple_of((base_ref[which] * PARTS + part) * step, step)
    for slot in range(w_ref.shape[0]):
        for last in range(SIDE):
            for plane in range(SIDE):
                piece = pieces[last][plane, slot] if source == "own" else pieces[plane][last, slot]
                line = (last * SIDE + plane) * granule
                rows_ref[line : line + granule] = piece[:, :step]
                if weigh:
                    info = piece[:, step:].astype(jnp.float32)
                    code = (CAP * (base_ref[2] + slot)).astype(jnp.float32)
                    lane = lax.broadcasted_iota(jnp.int32, info.shape, 1)
                    named = (info >= code) & (info < code + CAP) & (lane < META // 2)
                    value = pltpu.roll(info, META // 2, 1)
                    weight_ref[slot, line : line + granule] = jnp.sum(jnp.where(named, value, 0.0), axis=1, keepdims=True)
        total = jnp.dot(rows_ref[...], w_ref[slot, pl.ds(begin, step)], preferred_element_type=jnp.float32)
        if has_total:
            total = total + total_in[slot]
        if finish:
            total_ref[slot] = (jax.nn.silu(total[:, :columns]) * total[:, columns:]).astype(jnp.bfloat16)
        else:
            total_ref[slot] = total


def down_kernel(base_ref, hidden_ref, weight_ref, w_ref, *refs, part, turned):
    outs, added = refs[-SIDE:], refs[:-SIDE]
    granule, step = outs[0].shape[2:]
    which = 1 if turned else 0
    begin = pl.multiple_of((base_ref[which] * BACK + part) * step, step)
    for slot in range(hidden_ref.shape[0]):
        value = jnp.dot(hidden_ref[slot], w_ref[slot, :, pl.ds(begin, step)], preferred_element_type=jnp.float32)
        value = weight_ref[slot] * value
        for last in range(SIDE):
            for plane in range(SIDE):
                line = (last * SIDE + plane) * granule
                rows = value[line : line + granule]
                if turned:
                    outs[plane][last, slot] = rows.astype(jnp.bfloat16)
                else:
                    outs[last][plane, slot] = (rows + added[last][plane, slot].astype(jnp.float32)).astype(jnp.bfloat16)


def unpack_kernel(choice_ref, *refs):
    pieces, outs = refs[:SIDE], refs[SIDE:]
    for p in range(SIDE):
        values = jnp.concatenate([piece[p].reshape(-1, piece.shape[3]) for piece in pieces])
        dense = jnp.dot(choice_ref[p], values, preferred_element_type=jnp.float32)
        outs[p][...] = dense.astype(outs[p].dtype)


def whole(count):
    return [pl.BlockSpec(memory_space=pltpu.VMEM)] * count


def params(mebibytes=12):
    return pltpu.CompilerParams(vmem_limit_bytes=mebibytes * 2**20)


def cost(flops, read):
    return pl.CostEstimate(flops=int(flops), bytes_accessed=int(read), transcendentals=0)


def shards(tokens, expert_ids, gate_weights, placement, w_gate, w_up, w_down):
    tok_count, width = tokens.shape
    top = expert_ids.shape[1]
    per_device = w_gate.shape[0]
    half = width // 2
    step = half // PARTS
    core = lax.axis_index("dp") % 2
    first_core = core == 0
    own_slot = lax.axis_index("expert") * per_device
    local = jnp.arange(per_device, dtype=jnp.int32)
    scalar = [pl.BlockSpec(memory_space=pltpu.SMEM)]
    base = jnp.stack([core, 1 - core, own_slot]).astype(jnp.int32)

    carried = jax.ShapeDtypeStruct((tok_count, half + META), jnp.bfloat16)
    kept, sent = pl.pallas_call(
        prepare_kernel,
        grid=(1,),
        out_shape=[carried, carried],
        in_specs=scalar
        + [
            pl.BlockSpec(shape, lambda i: (0, 0))
            for shape in (tokens.shape, (top, tok_count), (top, tok_count), (1, placement.shape[0]))
        ],
        out_specs=whole(2),
        compiler_params=params(),
    )(base, tokens, expert_ids.T, gate_weights.T, placement.reshape(1, -1))
    got = sibling(sent)
    both = jnp.concatenate([jnp.where(first_core, kept, got), jnp.where(first_core, got, kept)])

    near_pieces = exchange_z([both] * SIDE, first_core)
    widths = [step + META] + [step] * (PARTS - 1)
    begins = [0] + [META + part * step for part in range(1, PARTS)]
    nears = [
        jnp.concatenate([piece[:, begin : begin + columns] for piece in near_pieces])
        for begin, columns in zip(begins, widths)
    ]
    near_count = nears[0].shape[0]

    lines = near_count // tok_count * CAP * per_device * SIDE
    masks = jnp.arange(SIDE, dtype=jnp.int32)
    moved = jnp.where(first_core, (masks & 1) * 2, masks * 4)
    slots = ((own_slot ^ moved)[:, None] + local[None, :]).reshape(-1)
    wanted = slots[:, None, None] * CAP + jnp.zeros((1, near_count // tok_count, 1), jnp.int32) + jnp.arange(CAP, dtype=jnp.int32)
    wanted = wanted.astype(jnp.float32).reshape(1, lines)
    granule = near_count // tok_count * CAP
    rows_of = lambda columns: jax.ShapeDtypeStruct((SIDE, per_device, granule, columns), jnp.bfloat16)
    rows_count, hidden_count = SIDE * SIDE * granule, w_gate.shape[2]

    def pack(part, chooser, planes):
        first = part == 0
        out_shape = [rows_of(widths[part])] * SIDE
        if first:
            out_shape.append(jax.ShapeDtypeStruct((SIDE, near_count, lines), jnp.bfloat16))
        return pl.pallas_call(
            functools.partial(pack_kernel, top=top, tok_count=tok_count, step=step, first=first),
            out_shape=out_shape,
            in_specs=whole(1 + SIDE),
            out_specs=whole(len(out_shape)),
            compiler_params=params(),
            cost_estimate=cost(2 * SIDE * lines * near_count * widths[part], 1e6),
        )(chooser, *planes)

    def project(source, part, pieces, total):
        weigh, finish = source == "own" and part == 0, source != "own" and part == PARTS - 1
        if finish:
            out_shape = [jax.ShapeDtypeStruct((per_device, rows_count, hidden_count), jnp.bfloat16)]
        else:
            out_shape = [jax.ShapeDtypeStruct((per_device, rows_count, 2 * hidden_count), jnp.float32)]
        if weigh:
            out_shape.append(jax.ShapeDtypeStruct((per_device, rows_count, 1), jnp.float32))
        operands = [*pieces, gate_up] + ([] if total is None else [total])
        return pl.pallas_call(
            functools.partial(
                gate_kernel, source=source, part=part, weigh=weigh, has_total=total is not None, finish=finish
            ),
            out_shape=out_shape,
            in_specs=scalar + whole(len(operands)),
            out_specs=whole(len(out_shape)),
            scratch_shapes=[pltpu.VMEM((rows_count, step), jnp.bfloat16)],
            compiler_params=params(),
            cost_estimate=cost(4 * per_device * rows_count * step * hidden_count, 4e6),
        )(base, *operands)

    total = choice = None
    for part in range(PARTS):
        planes = exchange([nears[part]] * SIDE, "yx")
        if part == 0:
            *packed, choice = pack(part, wanted, planes)
        else:
            packed = pack(part, choice, planes)
        if part == 0:
            gate_w, up_w, _ = lax.optimization_barrier((w_gate, w_up, packed[0]))
            gate_up = pl.pallas_call(
                fetch_kernel,
                out_shape=jax.ShapeDtypeStruct((*w_gate.shape[:2], 2 * w_gate.shape[2]), w_gate.dtype),
                in_specs=[pl.BlockSpec(memory_space=pltpu.HBM)] * 2,
                out_specs=pl.BlockSpec(memory_space=pltpu.VMEM),
                scratch_shapes=[pltpu.SemaphoreType.DMA((2,))],
                compiler_params=params(),
                cost_estimate=cost(0, 12e6),
            )(gate_w, up_w)
        own = exchange(packed, "xy")
        own[1], gate_up = lax.optimization_barrier((own[1], gate_up))
        found = project("own", part, own, total)
        if part == 0:
            total, weight = found
        else:
            [total] = found
        [total] = project("sibling", part, [sibling(piece) for piece in own], total)
    hidden = total

    back_step = half // BACK

    def down(hidden, part, turned, added):
        return pl.pallas_call(
            functools.partial(down_kernel, part=part, turned=turned),
            out_shape=[rows_of(back_step)] * SIDE,
            in_specs=scalar + whole(3 + len(added)),
            out_specs=whole(SIDE),
            compiler_params=params(),
            cost_estimate=cost(2 * per_device * rows_count * back_step * hidden_count, 5e6),
        )(base, hidden, weight, w_down, *added)

    sums = []
    for part in range(BACK):
        added = [sibling(piece) for piece in down(hidden, part, True, [])]
        mine = down(hidden, part, False, added)
        hidden, _ = lax.optimization_barrier((hidden, mine[0]))
        values = exchange(mine, "xy")
        kinds = [jnp.float32] + [jnp.bfloat16] * (SIDE - 1)
        dense = pl.pallas_call(
            unpack_kernel,
            out_shape=[jax.ShapeDtypeStruct((near_count, back_step), kind) for kind in kinds],
            in_specs=whole(1 + SIDE),
            out_specs=whole(SIDE),
            compiler_params=params(),
        )(choice, *values)
        sums.append(sum(piece.astype(jnp.float32) for piece in exchange(dense, "yx")))
    total = jnp.concatenate(sums, axis=1).reshape(SIDE, -1, half)
    sent = [total[0]] + [total[j].astype(jnp.bfloat16) for j in (1, 2, 3)]
    sent = exchange_z(sent, first_core)
    total = sum(piece.astype(jnp.float32) for piece in sent).astype(jnp.bfloat16).reshape(2, tok_count, half)
    kept = jnp.where(first_core, total[0], total[1])
    got = sibling(jnp.where(first_core, total[1], total[0]))
    return jnp.concatenate([jnp.where(first_core, kept, got), jnp.where(first_core, got, kept)], axis=1)


def solution(mesh):
    in_specs = (
        P(AXES, None),
        P(AXES, None),
        P(AXES, None),
        P(),
        P("expert", None, "dp"),
        P("expert", None, "dp"),
        P("expert", "dp", None),
    )
    return jax.shard_map(shards, mesh=mesh, in_specs=in_specs, out_specs=P(AXES, None), check_vma=False)
```

```python
import functools

import jax
import jax.numpy as jnp
from jax import lax
from jax.experimental import pallas as pl
from jax.experimental.pallas import tpu as pltpu
from jax.sharding import PartitionSpec as P

AXES = ("expert", "dp")
SIDE = 4
META = 128
CAP = 4
BACK = 2


def place(z, y, x, core):
    return ((z * SIDE + y) * 2 + x % 2) * 4 + (x // 2) * 2 + core


def partners(axes, masks):
    masks = (masks, masks) if isinstance(masks, int) else masks
    pairs = []
    for z in range(SIDE):
        for y in range(SIDE):
            for x in range(SIDE):
                for core in range(2):
                    other = [z, y, x]
                    other["zyx".index(axes[core])] ^= masks[core]
                    pairs.append((place(z, y, x, core), place(*other, core)))
    return pairs


def exchange(value, axes):
    over = lax.ppermute(value[2], AXES, partners(axes, 2))
    one, three = (lax.ppermute(value[j], AXES, partners(axes, j)) for j in (1, 3))
    return [value[0], one, over, three]


def exchange_z(value, first_core):
    over = lax.ppermute(value[2], AXES, partners("zz", 2))
    near = lax.ppermute(jnp.where(first_core, value[1], value[3]), AXES, partners("zz", (1, 3)))
    far = lax.ppermute(jnp.where(first_core, value[3], value[1]), AXES, partners("zz", (3, 1)))
    return [value[0], jnp.where(first_core, near, far), over, jnp.where(first_core, far, near)]


def sibling(value):
    pairs = [(i, i ^ 1) for i in range(SIDE**3 * 2)]
    return lax.ppermute(value, AXES, pairs)


def prepare_kernel(core_ref, tokens_ref, ids_ref, weights_ref, placement_ref, kept_ref, sent_ref):
    top, count = ids_ref.shape
    width = tokens_ref.shape[1]
    half = width // 2
    slot_count = placement_ref.shape[1]
    lanes = lax.broadcasted_iota(jnp.int32, (count, slot_count), 1)
    placement = placement_ref[...].astype(jnp.float32)
    line = lax.broadcasted_iota(jnp.int32, (count, count), 0)
    column = lax.broadcasted_iota(jnp.int32, (count, count), 1)
    diagonal = line == column
    slots = []
    named = jnp.zeros((count, slot_count), jnp.float32)
    for k in range(top):
        ids = jnp.sum(jnp.where(diagonal, ids_ref[k : k + 1], 0), axis=1, keepdims=True)
        slot = jnp.sum(jnp.where(ids == lanes, placement, 0.0), axis=1, keepdims=True)
        slots.append(slot)
        named = jnp.where(lanes.astype(jnp.float32) == slot, 1.0, named)
    before = jnp.where(line > column, 1.0, 0.0)
    ranks = jnp.dot(before.astype(jnp.bfloat16), named.astype(jnp.bfloat16), preferred_element_type=jnp.float32)
    lane = lax.broadcasted_iota(jnp.int32, (count, META), 1)
    meta = jnp.full((count, META), -1.0, jnp.float32)
    for k in range(top):
        rank = jnp.sum(jnp.where(lanes.astype(jnp.float32) == slots[k], ranks, 0.0), axis=1, keepdims=True)
        weight = jnp.sum(jnp.where(diagonal, weights_ref[k : k + 1], 0.0), axis=1, keepdims=True)
        high = weight.astype(jnp.bfloat16).astype(jnp.float32)
        middle = (weight - high).astype(jnp.bfloat16).astype(jnp.float32)
        for turn, term in enumerate((high, middle, weight - high - middle)):
            at = turn * top + k
            meta = jnp.where(lane == at, slots[k] * CAP + rank, meta)
            meta = jnp.where(lane == META // 2 + at, term, meta)
    meta = meta.astype(jnp.bfloat16)
    for ref, own in ((kept_ref, True), (sent_ref, False)):
        begin = core_ref[0] * half if own else half - core_ref[0] * half
        begin = pl.multiple_of(begin, 128)
        ref[:, :half] = tokens_ref[:, pl.ds(begin, half)]
        ref[:, half:] = meta


def fetch_kernel(wanted_ref, gate_ref, up_ref, *refs, top, tok_count):
    planes, (both_ref, high_ref, middle_ref, sems) = refs[:SIDE], refs[SIDE:]
    columns = gate_ref.shape[2]
    copies = [
        pltpu.make_async_copy(ref, both_ref.at[:, :, pl.ds(i * columns, columns)], sems.at[i])
        for i, ref in enumerate((gate_ref, up_ref))
    ]
    for copy in copies:
        copy.start()
    wanted = wanted_ref[...]
    inside = same_block(planes[0].shape[0], wanted.shape[1], tok_count)
    for p in range(SIDE):
        info = planes[p][:, planes[p].shape[1] - META :].astype(jnp.float32)
        weighted = jnp.zeros(inside.shape, jnp.float32)
        for k in range(top):
            at = [META // 2 + turn * top + k for turn in range(3)]
            weight = info[:, at[0] : at[0] + 1] + info[:, at[1] : at[1] + 1] + info[:, at[2] : at[2] + 1]
            weighted = jnp.where(info[:, k : k + 1] == wanted, weight, weighted)
        weighted = jnp.where(inside, weighted, 0.0)
        high = weighted.astype(jnp.bfloat16)
        high_ref[p] = high
        middle_ref[p] = (weighted - high.astype(jnp.float32)).astype(jnp.bfloat16)
    for copy in copies:
        copy.wait()


def same_block(tokens, lines, tok_count):
    blocks = tokens // tok_count
    token_block = lax.broadcasted_iota(jnp.int32, (tokens, lines), 0) // tok_count
    return token_block == lax.broadcasted_iota(jnp.int32, (tokens, lines), 1) // CAP % blocks


def pack_kernel(wanted_ref, *refs, top, tok_count):
    planes, outs = refs[:SIDE], refs[SIDE:]
    wanted = wanted_ref[...]
    inside = same_block(planes[0].shape[0], wanted.shape[1], tok_count)
    share = wanted.shape[1] // SIDE
    half = outs[0].shape[3]
    for p in range(SIDE):
        codes = planes[p][:, half:].astype(jnp.float32)
        found = codes[:, :1] == wanted
        for k in range(1, top):
            found = found | (codes[:, k : k + 1] == wanted)
        take = jnp.where(found & inside, 1.0, 0.0).T.astype(jnp.bfloat16)
        rows = jnp.dot(take, planes[p][:, :half], preferred_element_type=jnp.float32).astype(jnp.bfloat16)
        for j in range(SIDE):
            outs[j][p] = rows[j * share : (j + 1) * share].reshape(outs[j].shape[1:])


def gate_kernel(base_ref, *refs, source):
    pieces, (w_ref, total_ref, rows_ref) = refs[:2], refs[2:]
    step = rows_ref.shape[1]
    begin = pl.multiple_of(base_ref[0 if source == "own" else 1] * step, step)
    count = rows_ref.shape[0] // 2
    for slot in range(w_ref.shape[0]):
        for i, piece in enumerate(pieces):
            for other in range(SIDE):
                line = i * count + other * piece.shape[2]
                rows_ref[line : line + piece.shape[2]] = piece[other, slot]
        total_ref[slot] = jnp.dot(rows_ref[...], w_ref[slot, pl.ds(begin, step)], preferred_element_type=jnp.float32)


def hidden_kernel(base_ref, *refs):
    pieces, (w_ref, own_0, own_1, sib_0, hidden_ref, rows_ref) = refs[:2], refs[2:]
    step = rows_ref.shape[1]
    begin = pl.multiple_of(base_ref[1] * step, step)
    granule, count, columns = pieces[0].shape[2], rows_ref.shape[0] // 2, w_ref.shape[2] // 2
    for slot in range(w_ref.shape[0]):
        for i, piece in enumerate(pieces):
            for last in range(SIDE):
                line = i * count + last * granule
                rows_ref[line : line + granule] = piece[last, slot]
        sib_1 = jnp.dot(rows_ref[...], w_ref[slot, pl.ds(begin, step)], preferred_element_type=jnp.float32)
        for last in range(SIDE):
            own = own_0 if last < 2 else own_1
            for plane in range(SIDE):
                line = last % 2 * count + plane * granule
                across = plane % 2 * count + last * granule
                sib = sib_0[slot, across : across + granule] if plane < 2 else sib_1[across : across + granule]
                total = own[slot, line : line + granule] + sib
                line = (last * SIDE + plane) * granule
                hidden = jax.nn.silu(total[:, :columns]) * total[:, columns:]
                hidden_ref[slot, line : line + granule] = hidden.astype(jnp.bfloat16)


def down_kernel(base_ref, hidden_ref, w_ref, *refs, part, turned):
    outs, added = refs[-SIDE:], refs[:-SIDE]
    granule, step = outs[0].shape[2:]
    which = 1 if turned else 0
    begin = pl.multiple_of((base_ref[which] * BACK + part) * step, step)
    for slot in range(hidden_ref.shape[0]):
        value = jnp.dot(hidden_ref[slot], w_ref[slot, :, pl.ds(begin, step)], preferred_element_type=jnp.float32)
        for last in range(SIDE):
            for plane in range(SIDE):
                line = (last * SIDE + plane) * granule
                rows = value[line : line + granule]
                if turned:
                    outs[plane][last, slot] = rows.astype(jnp.bfloat16)
                else:
                    outs[last][plane, slot] = (rows + added[last][plane, slot].astype(jnp.float32)).astype(jnp.bfloat16)


def unpack_kernel(high_ref, middle_ref, *refs):
    pieces, outs = refs[:SIDE], refs[SIDE:]
    for p in range(SIDE):
        values = jnp.concatenate([piece[p].reshape(-1, piece.shape[3]) for piece in pieces])
        dense = jnp.dot(high_ref[p], values, preferred_element_type=jnp.float32)
        dense += jnp.dot(middle_ref[p], values, preferred_element_type=jnp.float32)
        outs[p][...] = dense.astype(outs[p].dtype)


def whole(count):
    return [pl.BlockSpec(memory_space=pltpu.VMEM)] * count


def params(mebibytes=12):
    return pltpu.CompilerParams(vmem_limit_bytes=mebibytes * 2**20)


def cost(flops, read):
    return pl.CostEstimate(flops=int(flops), bytes_accessed=int(read), transcendentals=0)


def shards(tokens, expert_ids, gate_weights, placement, w_gate, w_up, w_down):
    tok_count, width = tokens.shape
    top = expert_ids.shape[1]
    per_device = w_gate.shape[0]
    half = width // 2
    core = lax.axis_index("dp") % 2
    first_core = core == 0
    own_slot = lax.axis_index("expert") * per_device
    local = jnp.arange(per_device, dtype=jnp.int32)
    scalar = [pl.BlockSpec(memory_space=pltpu.SMEM)]
    base = jnp.stack([core, 1 - core, own_slot]).astype(jnp.int32)

    carried = jax.ShapeDtypeStruct((tok_count, half + META), jnp.bfloat16)
    kept, sent = pl.pallas_call(
        prepare_kernel,
        grid=(1,),
        out_shape=[carried, carried],
        in_specs=scalar
        + [
            pl.BlockSpec(shape, lambda i: (0, 0))
            for shape in (tokens.shape, (top, tok_count), (top, tok_count), (1, placement.shape[0]))
        ],
        out_specs=whole(2),
        compiler_params=params(56),
    )(base, tokens, expert_ids.T, gate_weights.T, placement.reshape(1, -1))
    got = sibling(sent)
    both = jnp.concatenate([jnp.where(first_core, kept, got), jnp.where(first_core, got, kept)])

    near_pieces = exchange_z([both] * SIDE, first_core)
    near = jnp.concatenate(near_pieces)
    near_count = near.shape[0]

    lines = near_count // tok_count * CAP * per_device * SIDE
    masks = jnp.arange(SIDE, dtype=jnp.int32)
    moved = jnp.where(first_core, (masks & 1) * 2, masks * 4)
    slots = ((own_slot ^ moved)[:, None] + local[None, :]).reshape(-1)
    wanted = slots[:, None, None] * CAP + jnp.zeros((1, near_count // tok_count, 1), jnp.int32) + jnp.arange(CAP, dtype=jnp.int32)
    wanted = wanted.astype(jnp.float32).reshape(1, lines)
    granule = near_count // tok_count * CAP
    rows_of = lambda columns: jax.ShapeDtypeStruct((SIDE, per_device, granule, columns), jnp.bfloat16)
    rows_count, hidden_count = SIDE * SIDE * granule, w_gate.shape[2]

    planes = exchange([near] * SIDE, "yx")
    packed = pl.pallas_call(
        functools.partial(pack_kernel, top=top, tok_count=tok_count),
        out_shape=[rows_of(half)] * SIDE,
        in_specs=whole(1 + SIDE),
        out_specs=whole(SIDE),
        compiler_params=params(),
        cost_estimate=cost(2 * SIDE * lines * near_count * half, 1e6),
    )(wanted, *planes)
    own = exchange(packed, "xy")

    gate_w, up_w, _ = lax.optimization_barrier((w_gate, w_up, packed[0]))
    back_matrix = jax.ShapeDtypeStruct((SIDE, near_count, lines), jnp.bfloat16)
    gate_up, high, middle = pl.pallas_call(
        functools.partial(fetch_kernel, top=top, tok_count=tok_count),
        out_shape=[
            jax.ShapeDtypeStruct((*w_gate.shape[:2], 2 * w_gate.shape[2]), w_gate.dtype),
            back_matrix,
            back_matrix,
        ],
        in_specs=whole(1) + [pl.BlockSpec(memory_space=pltpu.HBM)] * 2 + whole(SIDE),
        out_specs=whole(3),
        scratch_shapes=[pltpu.SemaphoreType.DMA((2,))],
        compiler_params=params(),
        cost_estimate=cost(1, 1),
    )(wanted, gate_w, up_w, *planes)

    own[1], gate_up = lax.optimization_barrier((own[1], gate_up))

    def project(source, pieces):
        return pl.pallas_call(
            functools.partial(gate_kernel, source=source),
            out_shape=jax.ShapeDtypeStruct((per_device, rows_count // 2, 2 * hidden_count), jnp.float32),
            in_specs=scalar + whole(3),
            out_specs=pl.BlockSpec(memory_space=pltpu.VMEM),
            scratch_shapes=[pltpu.VMEM((rows_count // 2, half), jnp.bfloat16)],
            compiler_params=params(),
            cost_estimate=cost(1, 1),
        )(base, *pieces, gate_up)

    own_0 = project("own", own[:2])
    sib_0 = project("sibling", [sibling(piece) for piece in own[:2]])
    own[2], own_0 = lax.optimization_barrier((own[2], own_0))
    own_1 = project("own", own[2:])
    hidden = pl.pallas_call(
        hidden_kernel,
        out_shape=jax.ShapeDtypeStruct((per_device, rows_count, hidden_count), jnp.bfloat16),
        in_specs=scalar + whole(6),
        out_specs=pl.BlockSpec(memory_space=pltpu.VMEM),
        scratch_shapes=[pltpu.VMEM((rows_count // 2, half), jnp.bfloat16)],
        compiler_params=params(),
        cost_estimate=cost(2 * per_device * rows_count * half * hidden_count, 4e6),
    )(base, *[sibling(piece) for piece in own[2:]], gate_up, own_0, own_1, sib_0)

    back_step = half // BACK

    def down(hidden, part, turned, added):
        return pl.pallas_call(
            functools.partial(down_kernel, part=part, turned=turned),
            out_shape=[rows_of(back_step)] * SIDE,
            in_specs=scalar + whole(2 + len(added)),
            out_specs=whole(SIDE),
            compiler_params=params(),
            cost_estimate=cost(2 * per_device * rows_count * back_step * hidden_count, 5e6),
        )(base, hidden, w_down, *added)

    sent = [down(hidden, part, True, []) for part in range(BACK)]
    hidden, _ = lax.optimization_barrier((hidden, [piece for pieces in sent for piece in pieces[:1]]))
    sums = []
    for part in range(BACK):
        mine = down(hidden, part, False, [sibling(piece) for piece in sent[part]])
        values = exchange(mine, "xy")
        kinds = [jnp.float32] + [jnp.bfloat16] * (SIDE - 1)
        dense = pl.pallas_call(
            unpack_kernel,
            out_shape=[jax.ShapeDtypeStruct((near_count, back_step), kind) for kind in kinds],
            in_specs=whole(2 + SIDE),
            out_specs=whole(SIDE),
            compiler_params=params(),
        )(high, middle, *values)
        sums.append(sum(piece.astype(jnp.float32) for piece in exchange(dense, "yx")))
    total = jnp.concatenate(sums, axis=1).reshape(SIDE, -1, half)
    sent = [total[0]] + [total[j].astype(jnp.bfloat16) for j in (1, 2, 3)]
    sent = exchange_z(sent, first_core)
    total = sum(piece.astype(jnp.float32) for piece in sent).astype(jnp.bfloat16).reshape(2, tok_count, half)
    kept = jnp.where(first_core, total[0], total[1])
    got = sibling(jnp.where(first_core, total[1], total[0]))
    return jnp.concatenate([jnp.where(first_core, kept, got), jnp.where(first_core, got, kept)], axis=1)


def solution(mesh):
    in_specs = (
        P(AXES, None),
        P(AXES, None),
        P(AXES, None),
        P(),
        P("expert", None, "dp"),
        P("expert", None, "dp"),
        P("expert", "dp", None),
    )
    return jax.shard_map(shards, mesh=mesh, in_specs=in_specs, out_specs=P(AXES, None), check_vma=False)
```

```python
import functools

import jax
import jax.numpy as jnp
from jax import lax
from jax.experimental import pallas as pl
from jax.experimental.pallas import tpu as pltpu
from jax.sharding import PartitionSpec as P

AXES = ("expert", "dp")
SIDE = 4
META = 128
CAP = 4
BACK = 2
ORDER = (2, 1, 3, 0)
EARLY, LATE = (0, 1, 3), (2,)


def place(z, y, x, core):
    return ((z * SIDE + y) * 2 + x % 2) * 4 + (x // 2) * 2 + core


def partners(axes, masks):
    masks = (masks, masks) if isinstance(masks, int) else masks
    pairs = []
    for z in range(SIDE):
        for y in range(SIDE):
            for x in range(SIDE):
                for core in range(2):
                    other = [z, y, x]
                    other["zyx".index(axes[core])] ^= masks[core]
                    pairs.append((place(z, y, x, core), place(*other, core)))
    return pairs


def exchange(value, axes):
    over = lax.ppermute(value[2], AXES, partners(axes, 2))
    one, three = (lax.ppermute(value[j], AXES, partners(axes, j)) for j in (1, 3))
    return [value[0], one, over, three]


def exchange_z(value, first_core):
    over = lax.ppermute(value[2], AXES, partners("zz", 2))
    near = lax.ppermute(jnp.where(first_core, value[1], value[3]), AXES, partners("zz", (1, 3)))
    far = lax.ppermute(jnp.where(first_core, value[3], value[1]), AXES, partners("zz", (3, 1)))
    return [value[0], jnp.where(first_core, near, far), over, jnp.where(first_core, far, near)]


def sibling(value):
    pairs = [(i, i ^ 1) for i in range(SIDE**3 * 2)]
    return lax.ppermute(value, AXES, pairs)


def taken(pieces, order=ORDER):
    return [pieces[j] for j in order]


def placed(pieces, order=ORDER):
    return [pieces[order.index(j)] for j in range(SIDE)]


def prepare_kernel(core_ref, tokens_ref, ids_ref, weights_ref, placement_ref, kept_ref, sent_ref):
    top, count = ids_ref.shape
    width = tokens_ref.shape[1]
    half = width // 2
    slot_count = placement_ref.shape[1]
    lanes = lax.broadcasted_iota(jnp.int32, (count, slot_count), 1)
    placement = placement_ref[...].astype(jnp.float32)
    line = lax.broadcasted_iota(jnp.int32, (count, count), 0)
    column = lax.broadcasted_iota(jnp.int32, (count, count), 1)
    diagonal = line == column
    slots = []
    named = jnp.zeros((count, slot_count), jnp.float32)
    for k in range(top):
        ids = jnp.sum(jnp.where(diagonal, ids_ref[k : k + 1], 0), axis=1, keepdims=True)
        slot = jnp.sum(jnp.where(ids == lanes, placement, 0.0), axis=1, keepdims=True)
        slots.append(slot)
        named = jnp.where(lanes.astype(jnp.float32) == slot, 1.0, named)
    before = jnp.where(line > column, 1.0, 0.0)
    ranks = jnp.dot(before.astype(jnp.bfloat16), named.astype(jnp.bfloat16), preferred_element_type=jnp.float32)
    lane = lax.broadcasted_iota(jnp.int32, (count, META), 1)
    meta = jnp.full((count, META), -1.0, jnp.float32)
    for k in range(top):
        rank = jnp.sum(jnp.where(lanes.astype(jnp.float32) == slots[k], ranks, 0.0), axis=1, keepdims=True)
        weight = jnp.sum(jnp.where(diagonal, weights_ref[k : k + 1], 0.0), axis=1, keepdims=True)
        high = weight.astype(jnp.bfloat16).astype(jnp.float32)
        middle = (weight - high).astype(jnp.bfloat16).astype(jnp.float32)
        for turn, term in enumerate((high, middle, weight - high - middle)):
            at = turn * top + k
            meta = jnp.where(lane == at, slots[k] * CAP + rank, meta)
            meta = jnp.where(lane == META // 2 + at, term, meta)
    meta = meta.astype(jnp.bfloat16)
    for ref, own in ((kept_ref, True), (sent_ref, False)):
        begin = core_ref[0] * half if own else half - core_ref[0] * half
        begin = pl.multiple_of(begin, 128)
        ref[:, :half] = tokens_ref[:, pl.ds(begin, half)]
        ref[:, half:] = meta


def fetch_kernel(wanted_ref, gate_ref, up_ref, *refs, top, tok_count):
    planes, (both_ref, high_ref, middle_ref, sems) = placed(refs[:SIDE], ORDER[::-1]), refs[SIDE:]
    columns = gate_ref.shape[2]
    copies = [
        pltpu.make_async_copy(ref, both_ref.at[:, :, pl.ds(i * columns, columns)], sems.at[i])
        for i, ref in enumerate((gate_ref, up_ref))
    ]
    for copy in copies:
        copy.start()
    wanted = wanted_ref[...]
    inside = same_block(planes[0].shape[0], wanted.shape[1], tok_count)
    for p in range(SIDE):
        info = planes[p][:, planes[p].shape[1] - META :].astype(jnp.float32)
        weighted = jnp.zeros(inside.shape, jnp.float32)
        for k in range(top):
            at = [META // 2 + turn * top + k for turn in range(3)]
            weight = info[:, at[0] : at[0] + 1] + info[:, at[1] : at[1] + 1] + info[:, at[2] : at[2] + 1]
            weighted = jnp.where(info[:, k : k + 1] == wanted, weight, weighted)
        weighted = jnp.where(inside, weighted, 0.0)
        high = weighted.astype(jnp.bfloat16)
        high_ref[p] = high
        middle_ref[p] = (weighted - high.astype(jnp.float32)).astype(jnp.bfloat16)
    for copy in copies:
        copy.wait()


def same_block(tokens, lines, tok_count):
    blocks = tokens // tok_count
    token_block = lax.broadcasted_iota(jnp.int32, (tokens, lines), 0) // tok_count
    return token_block == lax.broadcasted_iota(jnp.int32, (tokens, lines), 1) // CAP % blocks


def pack_kernel(wanted_ref, *refs, top, tok_count):
    planes, outs = placed(refs[:SIDE], ORDER[::-1]), refs[SIDE:]
    wanted = wanted_ref[...]
    inside = same_block(planes[0].shape[0], wanted.shape[1], tok_count)
    share = wanted.shape[1] // SIDE
    half = outs[0].shape[3]
    for p in range(SIDE):
        codes = planes[p][:, half:].astype(jnp.float32)
        found = codes[:, :1] == wanted
        for k in range(1, top):
            found = found | (codes[:, k : k + 1] == wanted)
        take = jnp.where(found & inside, 1.0, 0.0).T.astype(jnp.bfloat16)
        rows = jnp.dot(take, planes[p][:, :half], preferred_element_type=jnp.float32).astype(jnp.bfloat16)
        for j in range(SIDE):
            outs[j][p] = rows[j * share : (j + 1) * share].reshape(outs[j].shape[1:])


def gate_kernel(base_ref, *refs, source):
    pieces, (w_ref, total_ref, rows_ref) = refs[:-3], refs[-3:]
    for slot in range(w_ref.shape[0]):
        total_ref[slot] = products(base_ref, slot, pieces, w_ref, rows_ref, source)


def products(base_ref, slot, pieces, w_ref, rows_ref, source):
    step = rows_ref.shape[1]
    begin = pl.multiple_of(base_ref[0 if source == "own" else 1] * step, step)
    granule = pieces[0].shape[2]
    for i, piece in enumerate(pieces):
        for other in range(SIDE):
            line = (i * SIDE + other) * granule
            rows_ref[line : line + granule] = piece[other, slot]
    return jnp.dot(rows_ref[...], w_ref[slot, pl.ds(begin, step)], preferred_element_type=jnp.float32)


def hidden_kernel(base_ref, *refs):
    pieces, (w_ref, own_early, own_late, sib_early, hidden_ref, rows_ref) = refs[: len(LATE)], refs[len(LATE) :]
    granule, columns = pieces[0].shape[2], w_ref.shape[2] // 2
    for slot in range(w_ref.shape[0]):
        sib_late = products(base_ref, slot, pieces, w_ref, rows_ref, "sibling")
        for last in range(SIDE):
            for plane in range(SIDE):
                own = own_early if last in EARLY else own_late
                line = ((EARLY if last in EARLY else LATE).index(last) * SIDE + plane) * granule
                total = own[slot, line : line + granule]
                line = ((EARLY if plane in EARLY else LATE).index(plane) * SIDE + last) * granule
                total += sib_early[slot, line : line + granule] if plane in EARLY else sib_late[line : line + granule]
                line = (last * SIDE + plane) * granule
                hidden = jax.nn.silu(total[:, :columns]) * total[:, columns:]
                hidden_ref[slot, line : line + granule] = hidden.astype(jnp.bfloat16)


def down_kernel(base_ref, hidden_ref, w_ref, *refs, part, turned):
    outs, added = refs[-SIDE:], refs[:-SIDE]
    granule, step = outs[0].shape[2:]
    which = 1 if turned else 0
    begin = pl.multiple_of((base_ref[which] * BACK + part) * step, step)
    for slot in range(hidden_ref.shape[0]):
        value = jnp.dot(hidden_ref[slot], w_ref[slot, :, pl.ds(begin, step)], preferred_element_type=jnp.float32)
        for last in range(SIDE):
            for plane in range(SIDE):
                line = (last * SIDE + plane) * granule
                rows = value[line : line + granule]
                if turned:
                    outs[plane][last, slot] = rows.astype(jnp.bfloat16)
                else:
                    outs[last][plane, slot] = (rows + added[last][plane, slot].astype(jnp.float32)).astype(jnp.bfloat16)


def unpack_kernel(high_ref, middle_ref, *refs):
    pieces, outs = placed(refs[:SIDE]), refs[SIDE:]
    for p in range(SIDE):
        values = jnp.concatenate([piece[p].reshape(-1, piece.shape[3]) for piece in pieces])
        dense = jnp.dot(high_ref[p], values, preferred_element_type=jnp.float32)
        dense += jnp.dot(middle_ref[p], values, preferred_element_type=jnp.float32)
        outs[p][...] = dense.astype(outs[p].dtype)


def whole(count):
    return [pl.BlockSpec(memory_space=pltpu.VMEM)] * count


def params(mebibytes=12):
    return pltpu.CompilerParams(vmem_limit_bytes=mebibytes * 2**20)


def cost(flops, read):
    return pl.CostEstimate(flops=int(flops), bytes_accessed=int(read), transcendentals=0)


def shards(tokens, expert_ids, gate_weights, placement, w_gate, w_up, w_down):
    tok_count, width = tokens.shape
    top = expert_ids.shape[1]
    per_device = w_gate.shape[0]
    half = width // 2
    core = lax.axis_index("dp") % 2
    first_core = core == 0
    own_slot = lax.axis_index("expert") * per_device
    local = jnp.arange(per_device, dtype=jnp.int32)
    scalar = [pl.BlockSpec(memory_space=pltpu.SMEM)]
    base = jnp.stack([core, 1 - core, own_slot]).astype(jnp.int32)

    carried = jax.ShapeDtypeStruct((tok_count, half + META), jnp.bfloat16)
    kept, sent = pl.pallas_call(
        prepare_kernel,
        grid=(1,),
        out_shape=[carried, carried],
        in_specs=scalar
        + [
            pl.BlockSpec(shape, lambda i: (0, 0))
            for shape in (tokens.shape, (top, tok_count), (top, tok_count), (1, placement.shape[0]))
        ],
        out_specs=whole(2),
        compiler_params=params(56),
    )(base, tokens, expert_ids.T, gate_weights.T, placement.reshape(1, -1))
    got = sibling(sent)
    both = jnp.concatenate([jnp.where(first_core, kept, got), jnp.where(first_core, got, kept)])

    near_pieces = exchange_z([both] * SIDE, first_core)
    near = jnp.concatenate(near_pieces)
    near_count = near.shape[0]

    lines = near_count // tok_count * CAP * per_device * SIDE
    masks = jnp.arange(SIDE, dtype=jnp.int32)
    moved = jnp.where(first_core, (masks & 1) * 2, masks * 4)
    slots = ((own_slot ^ moved)[:, None] + local[None, :]).reshape(-1)
    wanted = slots[:, None, None] * CAP + jnp.zeros((1, near_count // tok_count, 1), jnp.int32) + jnp.arange(CAP, dtype=jnp.int32)
    wanted = wanted.astype(jnp.float32).reshape(1, lines)
    granule = near_count // tok_count * CAP
    rows_of = lambda columns: jax.ShapeDtypeStruct((SIDE, per_device, granule, columns), jnp.bfloat16)
    rows_count, hidden_count = SIDE * SIDE * granule, w_gate.shape[2]

    planes = exchange([near] * SIDE, "yx")
    packed = pl.pallas_call(
        functools.partial(pack_kernel, top=top, tok_count=tok_count),
        out_shape=[rows_of(half)] * SIDE,
        in_specs=whole(1 + SIDE),
        out_specs=whole(SIDE),
        compiler_params=params(),
        cost_estimate=cost(2 * SIDE * lines * near_count * half, 1e6),
    )(wanted, *taken(planes, ORDER[::-1]))
    own = exchange(packed, "xy")

    gate_w, up_w, _ = lax.optimization_barrier((w_gate, w_up, packed[0]))
    back_matrix = jax.ShapeDtypeStruct((SIDE, near_count, lines), jnp.bfloat16)
    gate_up, high, middle = pl.pallas_call(
        functools.partial(fetch_kernel, top=top, tok_count=tok_count),
        out_shape=[
            jax.ShapeDtypeStruct((*w_gate.shape[:2], 2 * w_gate.shape[2]), w_gate.dtype),
            back_matrix,
            back_matrix,
        ],
        in_specs=whole(1) + [pl.BlockSpec(memory_space=pltpu.HBM)] * 2 + whole(SIDE),
        out_specs=whole(3),
        scratch_shapes=[pltpu.SemaphoreType.DMA((2,))],
        compiler_params=params(),
        cost_estimate=cost(1, 1),
    )(wanted, gate_w, up_w, *taken(planes, ORDER[::-1]))

    own[1], gate_up = lax.optimization_barrier((own[1], gate_up))

    def project(source, pieces):
        count = len(pieces) * SIDE * granule
        return pl.pallas_call(
            functools.partial(gate_kernel, source=source),
            out_shape=jax.ShapeDtypeStruct((per_device, count, 2 * hidden_count), jnp.float32),
            in_specs=scalar + whole(len(pieces) + 1),
            out_specs=pl.BlockSpec(memory_space=pltpu.VMEM),
            scratch_shapes=[pltpu.VMEM((count, half), jnp.bfloat16)],
            compiler_params=params(),
            cost_estimate=cost(1, 1),
        )(base, *pieces, gate_up)

    own_early = project("own", [own[j] for j in EARLY])
    sib_early = project("sibling", [sibling(own[j]) for j in EARLY])
    own[2], own_early, sib_early = lax.optimization_barrier((own[2], own_early, sib_early))
    own_late = project("own", [own[j] for j in LATE])
    hidden = pl.pallas_call(
        hidden_kernel,
        out_shape=jax.ShapeDtypeStruct((per_device, rows_count, hidden_count), jnp.bfloat16),
        in_specs=scalar + whole(4 + len(LATE)),
        out_specs=pl.BlockSpec(memory_space=pltpu.VMEM),
        scratch_shapes=[pltpu.VMEM((len(LATE) * SIDE * granule, half), jnp.bfloat16)],
        compiler_params=params(),
        cost_estimate=cost(2 * per_device * rows_count * half * hidden_count, 4e6),
    )(base, *[sibling(own[j]) for j in LATE], gate_up, own_early, own_late, sib_early)

    back_step = half // BACK

    def down(hidden, part, turned, added):
        return pl.pallas_call(
            functools.partial(down_kernel, part=part, turned=turned),
            out_shape=[rows_of(back_step)] * SIDE,
            in_specs=scalar + whole(2 + len(added)),
            out_specs=whole(SIDE),
            compiler_params=params(),
            cost_estimate=cost(2 * per_device * rows_count * back_step * hidden_count, 5e6),
        )(base, hidden, w_down, *added)

    sent = [down(hidden, part, True, []) for part in range(BACK)]
    hidden, _ = lax.optimization_barrier((hidden, [piece for pieces in sent for piece in pieces[:1]]))
    sums = []
    for part in range(BACK):
        mine = down(hidden, part, False, [sibling(piece) for piece in sent[part]])
        values = exchange(mine, "xy")
        kinds = [jnp.float32] + [jnp.bfloat16] * (SIDE - 1)
        dense = pl.pallas_call(
            unpack_kernel,
            out_shape=[jax.ShapeDtypeStruct((near_count, back_step), kind) for kind in kinds],
            in_specs=whole(2 + SIDE),
            out_specs=whole(SIDE),
            compiler_params=params(),
        )(high, middle, *taken(values))
        sums.append(sum(piece.astype(jnp.float32) for piece in taken(exchange(dense, "yx"))))
    total = jnp.concatenate(sums, axis=1).reshape(SIDE, -1, half)
    sent = [total[0]] + [total[j].astype(jnp.bfloat16) for j in (1, 2, 3)]
    sent = exchange_z(sent, first_core)
    total = sum(piece.astype(jnp.float32) for piece in taken(sent)).astype(jnp.bfloat16).reshape(2, tok_count, half)
    kept = jnp.where(first_core, total[0], total[1])
    got = sibling(jnp.where(first_core, total[1], total[0]))
    return jnp.concatenate([jnp.where(first_core, kept, got), jnp.where(first_core, got, kept)], axis=1)


def solution(mesh):
    in_specs = (
        P(AXES, None),
        P(AXES, None),
        P(AXES, None),
        P(),
        P("expert", None, "dp"),
        P("expert", None, "dp"),
        P("expert", "dp", None),
    )
    return jax.shard_map(shards, mesh=mesh, in_specs=in_specs, out_specs=P(AXES, None), check_vma=False)
```

```python
import functools

import jax
import jax.numpy as jnp
from jax import lax
from jax.experimental import pallas as pl
from jax.experimental.pallas import tpu as pltpu
from jax.sharding import PartitionSpec as P

AXES = ("expert", "dp")
SIDE = 4
META = 128
CAP = 4
BACK = 2
ORDER = (2, 1, 3, 0)
EARLY, LATE = (0, 1, 3), (2,)


def place(z, y, x, core):
    return ((z * SIDE + y) * 2 + x % 2) * 4 + (x // 2) * 2 + core


def partners(axes, masks):
    masks = (masks, masks) if isinstance(masks, int) else masks
    pairs = []
    for z in range(SIDE):
        for y in range(SIDE):
            for x in range(SIDE):
                for core in range(2):
                    other = [z, y, x]
                    other["zyx".index(axes[core])] ^= masks[core]
                    pairs.append((place(z, y, x, core), place(*other, core)))
    return pairs


def exchange(value, axes):
    over = lax.ppermute(value[2], AXES, partners(axes, 2))
    one, three = (lax.ppermute(value[j], AXES, partners(axes, j)) for j in (1, 3))
    return [value[0], one, over, three]


def exchange_z(value, first_core):
    over = lax.ppermute(value[2], AXES, partners("zz", 2))
    near = lax.ppermute(jnp.where(first_core, value[1], value[3]), AXES, partners("zz", (1, 3)))
    far = lax.ppermute(jnp.where(first_core, value[3], value[1]), AXES, partners("zz", (3, 1)))
    return [value[0], jnp.where(first_core, near, far), over, jnp.where(first_core, far, near)]


def sibling(value):
    pairs = [(i, i ^ 1) for i in range(SIDE**3 * 2)]
    return lax.ppermute(value, AXES, pairs)


def taken(pieces, order=ORDER):
    return [pieces[j] for j in order]


def placed(pieces, order=ORDER):
    return [pieces[order.index(j)] for j in range(SIDE)]


def prepare_kernel(core_ref, tokens_ref, ids_ref, weights_ref, placement_ref, kept_ref, sent_ref):
    top, count = ids_ref.shape
    width = tokens_ref.shape[1]
    half = width // 2
    slot_count = placement_ref.shape[1]
    lanes = lax.broadcasted_iota(jnp.int32, (count, slot_count), 1)
    placement = placement_ref[...].astype(jnp.float32)
    line = lax.broadcasted_iota(jnp.int32, (count, count), 0)
    column = lax.broadcasted_iota(jnp.int32, (count, count), 1)
    diagonal = line == column
    slots = []
    named = jnp.zeros((count, slot_count), jnp.float32)
    for k in range(top):
        ids = jnp.sum(jnp.where(diagonal, ids_ref[k : k + 1], 0), axis=1, keepdims=True)
        slot = jnp.sum(jnp.where(ids == lanes, placement, 0.0), axis=1, keepdims=True)
        slots.append(slot)
        named = jnp.where(lanes.astype(jnp.float32) == slot, 1.0, named)
    before = jnp.where(line > column, 1.0, 0.0)
    ranks = jnp.dot(before.astype(jnp.bfloat16), named.astype(jnp.bfloat16), preferred_element_type=jnp.float32)
    lane = lax.broadcasted_iota(jnp.int32, (count, META), 1)
    meta = jnp.full((count, META), -1.0, jnp.float32)
    for k in range(top):
        rank = jnp.sum(jnp.where(lanes.astype(jnp.float32) == slots[k], ranks, 0.0), axis=1, keepdims=True)
        weight = jnp.sum(jnp.where(diagonal, weights_ref[k : k + 1], 0.0), axis=1, keepdims=True)
        high = weight.astype(jnp.bfloat16).astype(jnp.float32)
        middle = (weight - high).astype(jnp.bfloat16).astype(jnp.float32)
        for turn, term in enumerate((high, middle, weight - high - middle)):
            at = turn * top + k
            meta = jnp.where(lane == at, slots[k] * CAP + rank, meta)
            meta = jnp.where(lane == META // 2 + at, term, meta)
    meta = meta.astype(jnp.bfloat16)
    for ref, own in ((kept_ref, True), (sent_ref, False)):
        begin = core_ref[0] * half if own else half - core_ref[0] * half
        begin = pl.multiple_of(begin, 128)
        ref[:, :half] = tokens_ref[:, pl.ds(begin, half)]
        ref[:, half:] = meta


def fetch_kernel(wanted_ref, gate_ref, up_ref, *refs, top, tok_count):
    planes, (both_ref, high_ref, middle_ref, sems) = placed(refs[:SIDE], ORDER[::-1]), refs[SIDE:]
    columns = gate_ref.shape[2]
    copies = [
        pltpu.make_async_copy(ref, both_ref.at[:, :, pl.ds(i * columns, columns)], sems.at[i])
        for i, ref in enumerate((gate_ref, up_ref))
    ]
    for copy in copies:
        copy.start()
    wanted = wanted_ref[...]
    inside = same_block(planes[0].shape[0], wanted.shape[1], tok_count)
    for p in range(SIDE):
        info = planes[p][:, planes[p].shape[1] - META :].astype(jnp.float32)
        weighted = jnp.zeros(inside.shape, jnp.float32)
        for k in range(top):
            at = [META // 2 + turn * top + k for turn in range(3)]
            weight = info[:, at[0] : at[0] + 1] + info[:, at[1] : at[1] + 1] + info[:, at[2] : at[2] + 1]
            weighted = jnp.where(info[:, k : k + 1] == wanted, weight, weighted)
        weighted = jnp.where(inside, weighted, 0.0)
        high = weighted.astype(jnp.bfloat16)
        high_ref[p] = high
        middle_ref[p] = (weighted - high.astype(jnp.float32)).astype(jnp.bfloat16)
    for copy in copies:
        copy.wait()


def same_block(tokens, lines, tok_count):
    blocks = tokens // tok_count
    token_block = lax.broadcasted_iota(jnp.int32, (tokens, lines), 0) // tok_count
    return token_block == lax.broadcasted_iota(jnp.int32, (tokens, lines), 1) // CAP % blocks


def pack_kernel(wanted_ref, *refs, top, tok_count):
    planes, outs = placed(refs[:SIDE], ORDER[::-1]), refs[SIDE:]
    wanted = wanted_ref[...]
    inside = same_block(planes[0].shape[0], wanted.shape[1], tok_count)
    share = wanted.shape[1] // SIDE
    half = outs[0].shape[3]
    for p in range(SIDE):
        codes = planes[p][:, half:].astype(jnp.float32)
        found = codes[:, :1] == wanted
        for k in range(1, top):
            found = found | (codes[:, k : k + 1] == wanted)
        take = jnp.where(found & inside, 1.0, 0.0).T.astype(jnp.bfloat16)
        rows = jnp.dot(take, planes[p][:, :half], preferred_element_type=jnp.float32).astype(jnp.bfloat16)
        for j in range(SIDE):
            outs[j][p] = rows[j * share : (j + 1) * share].reshape(outs[j].shape[1:])


def gate_kernel(base_ref, *refs, source):
    pieces, (w_ref, total_ref, rows_ref) = refs[:-3], refs[-3:]
    for slot in range(w_ref.shape[0]):
        total_ref[slot] = products(base_ref, slot, pieces, w_ref, rows_ref, source)


def products(base_ref, slot, pieces, w_ref, rows_ref, source):
    step = rows_ref.shape[1]
    begin = pl.multiple_of(base_ref[0 if source == "own" else 1] * step, step)
    granule = pieces[0].shape[2]
    for i, piece in enumerate(pieces):
        for other in range(SIDE):
            line = (i * SIDE + other) * granule
            rows_ref[line : line + granule] = piece[other, slot]
    return jnp.dot(rows_ref[...], w_ref[slot, pl.ds(begin, step)], preferred_element_type=jnp.float32)


def hidden_kernel(base_ref, *refs):
    pieces, (w_ref, own_early, own_late, sib_early, hidden_ref, rows_ref) = refs[: len(LATE)], refs[len(LATE) :]
    granule, columns = pieces[0].shape[2], w_ref.shape[2] // 2
    for slot in range(w_ref.shape[0]):
        sib_late = products(base_ref, slot, pieces, w_ref, rows_ref, "sibling")
        for last in range(SIDE):
            for plane in range(SIDE):
                own = own_early if last in EARLY else own_late
                line = ((EARLY if last in EARLY else LATE).index(last) * SIDE + plane) * granule
                total = own[slot, line : line + granule]
                line = ((EARLY if plane in EARLY else LATE).index(plane) * SIDE + last) * granule
                total += sib_early[slot, line : line + granule] if plane in EARLY else sib_late[line : line + granule]
                line = (last * SIDE + plane) * granule
                hidden = jax.nn.silu(total[:, :columns]) * total[:, columns:]
                hidden_ref[slot, line : line + granule] = hidden.astype(jnp.bfloat16)


def down_kernel(base_ref, hidden_ref, w_ref, *refs, part, turned):
    outs, added = refs[-SIDE:], refs[:-SIDE]
    granule, step = outs[0].shape[2:]
    which = 1 if turned else 0
    begin = pl.multiple_of((base_ref[which] * BACK + part) * step, step)
    for slot in range(hidden_ref.shape[0]):
        value = jnp.dot(hidden_ref[slot], w_ref[slot, :, pl.ds(begin, step)], preferred_element_type=jnp.float32)
        for last in range(SIDE):
            for plane in range(SIDE):
                line = (last * SIDE + plane) * granule
                rows = value[line : line + granule]
                if turned:
                    outs[plane][last, slot] = rows.astype(jnp.bfloat16)
                else:
                    outs[last][plane, slot] = (rows + added[last][plane, slot].astype(jnp.float32)).astype(jnp.bfloat16)


def unpack_kernel(high_ref, middle_ref, *refs):
    pieces, outs = placed(refs[:SIDE]), refs[SIDE:]
    for p in range(SIDE):
        values = jnp.concatenate([piece[p].reshape(-1, piece.shape[3]) for piece in pieces])
        dense = jnp.dot(high_ref[p], values, preferred_element_type=jnp.float32)
        dense += jnp.dot(middle_ref[p], values, preferred_element_type=jnp.float32)
        outs[p][...] = dense.astype(outs[p].dtype)


def whole(count):
    return [pl.BlockSpec(memory_space=pltpu.VMEM)] * count


def params(mebibytes=12):
    return pltpu.CompilerParams(vmem_limit_bytes=mebibytes * 2**20)


def cost(flops, read):
    return pl.CostEstimate(flops=int(flops), bytes_accessed=int(read), transcendentals=0)


def shards(tokens, expert_ids, gate_weights, placement, w_gate, w_up, w_down):
    tok_count, width = tokens.shape
    top = expert_ids.shape[1]
    per_device = w_gate.shape[0]
    half = width // 2
    core = lax.axis_index("dp") % 2
    first_core = core == 0
    own_slot = lax.axis_index("expert") * per_device
    local = jnp.arange(per_device, dtype=jnp.int32)
    scalar = [pl.BlockSpec(memory_space=pltpu.SMEM)]
    base = jnp.stack([core, 1 - core, own_slot]).astype(jnp.int32)

    carried = jax.ShapeDtypeStruct((tok_count, half + META), jnp.bfloat16)
    kept, sent = pl.pallas_call(
        prepare_kernel,
        grid=(1,),
        out_shape=[carried, carried],
        in_specs=scalar
        + [
            pl.BlockSpec(shape, lambda i: (0, 0))
            for shape in (tokens.shape, (top, tok_count), (top, tok_count), (1, placement.shape[0]))
        ],
        out_specs=whole(2),
        compiler_params=params(56),
    )(base, tokens, expert_ids.T, gate_weights.T, placement.reshape(1, -1))
    got = sibling(sent)
    both = jnp.concatenate([jnp.where(first_core, kept, got), jnp.where(first_core, got, kept)])

    near_pieces = exchange_z([both] * SIDE, first_core)
    near = jnp.concatenate(near_pieces)
    near_count = near.shape[0]

    lines = near_count // tok_count * CAP * per_device * SIDE
    masks = jnp.arange(SIDE, dtype=jnp.int32)
    moved = jnp.where(first_core, (masks & 1) * 2, masks * 4)
    slots = ((own_slot ^ moved)[:, None] + local[None, :]).reshape(-1)
    wanted = slots[:, None, None] * CAP + jnp.zeros((1, near_count // tok_count, 1), jnp.int32) + jnp.arange(CAP, dtype=jnp.int32)
    wanted = wanted.astype(jnp.float32).reshape(1, lines)
    granule = near_count // tok_count * CAP
    rows_of = lambda columns: jax.ShapeDtypeStruct((SIDE, per_device, granule, columns), jnp.bfloat16)
    rows_count, hidden_count = SIDE * SIDE * granule, w_gate.shape[2]

    planes = exchange([near] * SIDE, "yx")
    packed = pl.pallas_call(
        functools.partial(pack_kernel, top=top, tok_count=tok_count),
        out_shape=[rows_of(half)] * SIDE,
        in_specs=whole(1 + SIDE),
        out_specs=whole(SIDE),
        compiler_params=params(),
        cost_estimate=cost(2 * SIDE * lines * near_count * half, 1e6),
    )(wanted, *taken(planes, ORDER[::-1]))
    own = exchange(packed, "xy")

    gate_w, up_w, _ = lax.optimization_barrier((w_gate, w_up, packed[0]))
    back_matrix = jax.ShapeDtypeStruct((SIDE, near_count, lines), jnp.bfloat16)
    gate_up, high, middle = pl.pallas_call(
        functools.partial(fetch_kernel, top=top, tok_count=tok_count),
        out_shape=[
            jax.ShapeDtypeStruct((*w_gate.shape[:2], 2 * w_gate.shape[2]), w_gate.dtype),
            back_matrix,
            back_matrix,
        ],
        in_specs=whole(1) + [pl.BlockSpec(memory_space=pltpu.HBM)] * 2 + whole(SIDE),
        out_specs=whole(3),
        scratch_shapes=[pltpu.SemaphoreType.DMA((2,))],
        compiler_params=params(),
        cost_estimate=cost(1, 1),
    )(wanted, gate_w, up_w, *taken(planes, ORDER[::-1]))

    own[1], gate_up = lax.optimization_barrier((own[1], gate_up))

    def project(source, pieces):
        count = len(pieces) * SIDE * granule
        return pl.pallas_call(
            functools.partial(gate_kernel, source=source),
            out_shape=jax.ShapeDtypeStruct((per_device, count, 2 * hidden_count), jnp.float32),
            in_specs=scalar + whole(len(pieces) + 1),
            out_specs=pl.BlockSpec(memory_space=pltpu.VMEM),
            scratch_shapes=[pltpu.VMEM((count, half), jnp.bfloat16)],
            compiler_params=params(),
            cost_estimate=cost(1, 1),
        )(base, *pieces, gate_up)

    own_early = project("own", [own[j] for j in EARLY])
    sib_early = project("sibling", [sibling(own[j]) for j in EARLY])
    own[2], own_early, sib_early = lax.optimization_barrier((own[2], own_early, sib_early))
    own_late = project("own", [own[j] for j in LATE])
    hidden = pl.pallas_call(
        hidden_kernel,
        out_shape=jax.ShapeDtypeStruct((per_device, rows_count, hidden_count), jnp.bfloat16),
        in_specs=scalar + whole(4 + len(LATE)),
        out_specs=pl.BlockSpec(memory_space=pltpu.VMEM),
        scratch_shapes=[pltpu.VMEM((len(LATE) * SIDE * granule, half), jnp.bfloat16)],
        compiler_params=params(),
        cost_estimate=cost(2 * per_device * rows_count * half * hidden_count, 4e6),
    )(base, *[sibling(own[j]) for j in LATE], gate_up, own_early, own_late, sib_early)

    back_step = half // BACK

    def down(hidden, part, turned, added):
        return pl.pallas_call(
            functools.partial(down_kernel, part=part, turned=turned),
            out_shape=[rows_of(back_step)] * SIDE,
            in_specs=scalar + whole(2 + len(added)),
            out_specs=whole(SIDE),
            compiler_params=params(),
            cost_estimate=cost(2 * per_device * rows_count * back_step * hidden_count, 5e6),
        )(base, hidden, w_down, *added)

    sent = [down(hidden, part, True, []) for part in range(BACK)]
    hidden, _ = lax.optimization_barrier((hidden, [piece for pieces in sent for piece in pieces[:1]]))
    sums = []
    for part in range(BACK):
        mine = down(hidden, part, False, [sibling(piece) for piece in sent[part]])
        values = exchange(mine, "xy")
        kinds = [jnp.float32] + [jnp.bfloat16] * (SIDE - 1)
        dense = pl.pallas_call(
            unpack_kernel,
            out_shape=[jax.ShapeDtypeStruct((near_count, back_step), kind) for kind in kinds],
            in_specs=whole(2 + SIDE),
            out_specs=whole(SIDE),
            compiler_params=params(),
        )(high, middle, *taken(values))
        total = sum(piece.astype(jnp.float32) for piece in taken(exchange(dense, "yx"))).reshape(SIDE, -1, back_step)
        pieces = exchange_z([total[0]] + [total[j].astype(jnp.bfloat16) for j in (1, 2, 3)], first_core)
        sums.append(sum(piece.astype(jnp.float32) for piece in taken(pieces)))
    total = jnp.concatenate(sums, axis=1).astype(jnp.bfloat16).reshape(2, tok_count, half)
    kept = jnp.where(first_core, total[0], total[1])
    got = sibling(jnp.where(first_core, total[1], total[0]))
    return jnp.concatenate([jnp.where(first_core, kept, got), jnp.where(first_core, got, kept)], axis=1)


def solution(mesh):
    in_specs = (
        P(AXES, None),
        P(AXES, None),
        P(AXES, None),
        P(),
        P("expert", None, "dp"),
        P("expert", None, "dp"),
        P("expert", "dp", None),
    )
    return jax.shard_map(shards, mesh=mesh, in_specs=in_specs, out_specs=P(AXES, None), check_vma=False)
```
